32 devices in a mesh: group: 2 (over y), layer: 4 (over x, core), feat: 4 (over z).
Axes of the slice: x: 2, y: 2, z: 4, core: 2. Of those that a mesh axis runs over, the one named last changes fastest.
Arguments:
- inputs: bfloat16 [8, 4096, 1024], P(('group', 'layer'), 'feat'), parts along dimension 0, may hold values from -6 to 6
- targets: bfloat16 [8, 4096, 1024], P(('group', 'layer'), 'feat'), parts along dimension 0, may hold values from -6 to 6
- enc_weight: float32 [8, 128, 4096], P(('group', 'layer'), 'feat'), parts along dimension 0, may hold values from -0.09375 to 0.09375
- enc_bias: float32 [8, 128], P(('group', 'layer'), 'feat'), parts along dimension 0, may hold values from -1 to 0.5
- dec_weight: float32 [8, 4, 128, 4096], P(('group', 'layer'), None, 'feat'), parts along dimension 0, may hold values from -0.5 to 0.5
- dec_bias: float32 [8, 4096], P(('group', 'layer'), 'feat'), parts along dimension 0, may hold values from -3 to 3
- enc_moments: float32 [2, 8, 128, 4096], P(None, ('group', 'layer'), 'feat'), parts along dimension 1, as said below
- enc_bias_moments: float32 [2, 8, 128], P(None, ('group', 'layer'), 'feat'), parts along dimension 1, as said below
- dec_moments: float32 [2, 8, 4, 128, 4096], P(None, ('group', 'layer'), None, 'feat'), parts along dimension 1, as said below
- dec_bias_moments: float32 [2, 8, 4096], P(None, ('group', 'layer'), 'feat'), parts along dimension 1, as said below
- block_lists: int32 [8, 64, 128], P(('group', 'layer')), parts along dimension 0, may hold values from 0 to 255, as said below
- block_counts: int32 [8, 64], P(('group', 'layer')), parts along dimension 0, may hold values from 1 to 128, as said below
- slot_block: int32 [8], P(('group', 'layer')), parts along dimension 0, may hold values from 0 to 255
Outputs:
- enc_weight_new: float32 [8, 128, 4096], P(('group', 'layer'), 'feat'), parts along dimension 0
- enc_bias_new: float32 [8, 128], P(('group', 'layer'), 'feat'), parts along dimension 0
- dec_weight_new: float32 [8, 4, 128, 4096], P(('group', 'layer'), None, 'feat'), parts along dimension 0
- dec_bias_new: float32 [8, 4096], P(('group', 'layer'), 'feat'), parts along dimension 0
- enc_moments_new: float32 [2, 8, 128, 4096], P(None, ('group', 'layer'), 'feat'), parts along dimension 1
- enc_bias_moments_new: float32 [2, 8, 128], P(None, ('group', 'layer'), 'feat'), parts along dimension 1
- dec_moments_new: float32 [2, 8, 4, 128, 4096], P(None, ('group', 'layer'), None, 'feat'), parts along dimension 1
- dec_bias_moments_new: float32 [2, 8, 4096], P(None, ('group', 'layer'), 'feat'), parts along dimension 1
The draws below stay inside these ranges and needn't reach their ends.
There are 2 independent parts, one for each index of `group`. The reference program is written for one: setup_inputs(seed, part) draws one part's arguments, and reference() takes and returns one part's arrays. A program takes and returns all parts, laid end to end along the dimension named above; each array names one. Nothing has to cross between parts.
Inputs may be any that keep to these rules, and one draw needn't show every extreme that they name: `block_lists`: entries of one list are distinct block numbers; only the first block_counts entries of a list are live. `block_counts`: some layer and tile has all 128 entries live in every draw. `enc_moments`: the first moment is signed, the second positive. `enc_bias_moments`: the first moment is signed, the second positive. `dec_moments`: the first moment is signed, the second positive. `dec_bias_moments`: the first moment is signed, the second positive.
All inputs are finite; a program needn't handle non-finite values.
Results may differ from the reference program's by a relative error of at most 0.0003.
Values may be sent and summed in bfloat16 or wider, within the bound.
No kernel may reach another device: no remote copies, remote signals or barrier semaphores. Data moves between devices by JAX's collectives and lax.ppermute only.
A program may use at most 128 MiB of HBM per device.

```python
import math
import jax
import jax.numpy as jnp
from jax import lax

D = 4096
FEATS = 128
NBLK = 256
ACT = 128
ROWS = 1024
TILE = 16
REACH = 4
LAYERS = 4
TILES = 64


def moment_pair(key, shape, first_scale, lowest, highest_value):
    first_key, second_key = jax.random.split(key)
    first = first_scale * jax.random.normal(first_key, shape, jnp.float32)
    second = jnp.exp(jax.random.uniform(second_key, shape, jnp.float32, math.log(lowest), math.log(highest_value)))
    return jnp.stack([first, second]).astype(jnp.float32)


def draw_enc_moments(key, part):
    key = jax.random.fold_in(key, 21)
    return moment_pair(key, (LAYERS, FEATS, D), 5.0, 1.0, 100.0)


def draw_enc_bias_moments(key, part):
    key = jax.random.fold_in(key, 22)
    return moment_pair(key, (LAYERS, FEATS), 10.0, 10.0, 1000.0)


def draw_dec_moments(key, part):
    key = jax.random.fold_in(key, 23)
    return moment_pair(key, (LAYERS, REACH, FEATS, D), 1.0, 0.1, 10.0)


def draw_dec_bias_moments(key, part):
    key = jax.random.fold_in(key, 24)
    return moment_pair(key, (LAYERS, D), 2.0, 1.0, 100.0)


def draw_block_lists(key, part):
    key = jax.random.fold_in(key, 11)
    scores = jax.random.randint(key, (LAYERS, TILES, NBLK), 0, 1 << 20) * NBLK + jnp.arange(NBLK)[None, None, :]
    order = jnp.argsort(scores, axis=-1)
    return order[:, :, :ACT].astype(jnp.int32)


def draw_block_counts(key, part):
    key = jax.random.fold_in(key, 12)
    count_key, spot_key = jax.random.split(key)
    counts = jax.random.randint(count_key, (LAYERS * TILES,), 1, ACT + 1)
    spot = jax.random.randint(spot_key, (), 0, LAYERS * TILES)
    counts = jnp.where(jnp.arange(LAYERS * TILES) == spot, ACT, counts)
    return counts.reshape(LAYERS, TILES).astype(jnp.int32)


def set_ends(entries, stream_key, least, high):
    dims = entries.shape
    place = [jax.random.randint(jax.random.fold_in(stream_key, axis), (), 0, dims[axis]) for axis in range(len(dims))]
    entries = entries.at[tuple(place)].set(least)
    longest = dims.index(max(dims))
    place[longest] = (place[longest] + 1) % dims[longest]
    return entries.at[tuple(place)].set(high)


def block_scale(key, dims, pieces, smallest, largest):
    factor_of, own = 1.0, jax.random.fold_in(key, 6)
    for dim, parts in pieces:
        heights = jnp.exp(jax.random.uniform(jax.random.fold_in(own, dim), (parts,), jnp.float32, smallest / len(pieces), largest / len(pieces)))
        factor_of = factor_of * jnp.repeat(heights, dims[dim] // parts).reshape([-1 if axis == dim else 1 for axis in range(len(dims))])
    return factor_of


def normal_values(key, extent, width, most, shards=(), kind=jnp.bfloat16):
    array = width * jax.random.normal(key, extent, jnp.float32)
    if shards:
        array = array * block_scale(key, extent, shards, -0.22, 0.18)
    return jnp.clip(array, -most, most).astype(kind)


def setup_inputs(seed: int = 0, part: int = 0) -> dict:
    splits = jax.random.split(jax.random.key(seed), 14)
    own_keys = jax.random.split(jax.random.fold_in(splits[13], part), 14)
    inputs = normal_values(own_keys[0], (LAYERS, D, ROWS), 1.0, 6.0, ((0, 4), (1, 4)))
    targets = normal_values(own_keys[1], (LAYERS, D, ROWS), 1.0, 6.0, ((0, 4), (1, 4)))
    enc_weight = normal_values(own_keys[2], (LAYERS, FEATS, D), D ** -0.5, 0.09375, ((0, 4), (1, 4)), jnp.float32)
    enc_bias = jnp.clip(-1.0 + 1.5 * jax.random.uniform(own_keys[3], (LAYERS, FEATS), jnp.float32) ** block_scale(own_keys[3], (LAYERS, FEATS), ((0, 4), (1, 4)), -0.2, 0.2), -1.0, 0.5)
    dec_weight = normal_values(own_keys[4], (LAYERS, REACH, FEATS, D), FEATS ** -0.5, 0.5, ((0, 4), (2, 4)), jnp.float32)
    dec_bias = normal_values(own_keys[5], (LAYERS, D), 0.5, 3.0, ((0, 4), (1, 4)), jnp.float32)
    enc_moments = draw_enc_moments(jax.random.fold_in(jax.random.fold_in(splits[13], part), 71), part)
    enc_bias_moments = draw_enc_bias_moments(jax.random.fold_in(jax.random.fold_in(splits[13], part), 71), part)
    dec_moments = draw_dec_moments(jax.random.fold_in(jax.random.fold_in(splits[13], part), 71), part)
    dec_bias_moments = draw_dec_bias_moments(jax.random.fold_in(jax.random.fold_in(splits[13], part), 71), part)
    block_lists = draw_block_lists(jax.random.fold_in(jax.random.fold_in(splits[13], part), 71), part)
    block_counts = draw_block_counts(jax.random.fold_in(jax.random.fold_in(splits[13], part), 71), part)
    slot_block = set_ends(jax.random.randint(own_keys[12], (LAYERS,), 0, NBLK), jax.random.fold_in(own_keys[12], 1), 0, NBLK - 1).astype(jnp.int32)
    return dict(inputs=inputs, targets=targets, enc_weight=enc_weight, enc_bias=enc_bias, dec_weight=dec_weight, dec_bias=dec_bias, enc_moments=enc_moments, enc_bias_moments=enc_bias_moments, dec_moments=dec_moments, dec_bias_moments=dec_bias_moments, block_lists=block_lists, block_counts=block_counts, slot_block=slot_block)


beta_one = 0.9
beta_two = 0.999
learn_rate = 0.001
adam_eps = 1e-08
step_count = 100.0
highest = lax.Precision.HIGHEST

def adam_update(weight, moments, grad):
    first = beta_one * moments[0] + (1.0 - beta_one) * grad
    second = beta_two * moments[1] + (1.0 - beta_two) * grad * grad
    scaled_first = first / (1.0 - beta_one ** step_count)
    scaled_second = second / (1.0 - beta_two ** step_count)
    updated = weight - learn_rate * scaled_first / (jnp.sqrt(scaled_second) + adam_eps)
    return (updated, jnp.stack([first, second]))

def block_mask(block_lists, block_counts, slot_block):
    live = jnp.arange(ACT)[None, None, :] < block_counts[:, :, None]
    hits = (block_lists == slot_block[:, None, None]) & live
    tile_active = jnp.any(hits, axis=2).astype(jnp.float32)
    return jnp.repeat(tile_active, TILE, axis=1)[:, None, :]

def reference(inputs, targets, enc_weight, enc_bias, dec_weight, dec_bias, enc_moments, enc_bias_moments, dec_moments, dec_bias_moments, block_lists, block_counts, slot_block):
    active = block_mask(block_lists, block_counts, slot_block)
    inputs_wide = inputs.astype(jnp.float32)
    targets_wide = targets.astype(jnp.float32)
    pre = jnp.einsum('lfd,ldr->lfr', enc_weight, inputs_wide, precision=highest) + enc_bias[:, :, None]
    codes = jnp.maximum(pre, 0.0) * active
    stacked = []
    for offset in range(REACH):
        moved = jnp.concatenate([jnp.zeros((offset, FEATS, ROWS), jnp.float32), codes[:LAYERS - offset]], axis=0)
        stacked.append(moved)
    sources = jnp.stack(stacked, axis=1)
    recon = jnp.einsum('lkfd,lkfr->ldr', dec_weight, sources, precision=highest) + dec_bias[:, :, None]
    resid = recon - targets_wide
    grad_dec = jnp.einsum('lkfr,ldr->lkfd', sources, resid, precision=highest)
    grad_dec_bias = lax.optimization_barrier(jnp.sum(resid, axis=2))
    code_parts = jnp.einsum('lkfd,ldr->lkfr', dec_weight, resid, precision=highest)
    code_grad = jnp.zeros((LAYERS, FEATS, ROWS), jnp.float32)
    for offset in range(REACH):
        part = code_parts[:, offset]
        code_grad = code_grad + jnp.concatenate([part[offset:], jnp.zeros((offset, FEATS, ROWS), jnp.float32)], axis=0)
    pre_grad = code_grad * active * (pre > 0.0).astype(jnp.float32)
    grad_enc = jnp.einsum('lfr,ldr->lfd', pre_grad, inputs_wide, precision=highest)
    grad_enc_bias = lax.optimization_barrier(jnp.sum(pre_grad, axis=2))
    enc_new, enc_mom = adam_update(enc_weight, enc_moments, grad_enc)
    encb_new, encb_mom = adam_update(enc_bias, enc_bias_moments, grad_enc_bias)
    dec_new, dec_mom = adam_update(dec_weight, dec_moments, grad_dec)
    decb_new, decb_mom = adam_update(dec_bias, dec_bias_moments, grad_dec_bias)
    return (enc_new, encb_new, dec_new, decb_new, enc_mom, encb_mom, dec_mom, decb_mom)
```

```python
import jax
import jax.numpy as jnp
from jax import lax
from jax.sharding import PartitionSpec as P

beta_one = 0.9
beta_two = 0.999
learn_rate = 0.001
adam_eps = 1e-08
step_count = 100.0
highest = lax.Precision.HIGHEST
high = lax.Precision.HIGH


def shifted(value, axis, steps):
    count = lax.axis_size(axis)
    initial, last = (max(0, -steps), min(count, count - steps))
    return lax.ppermute(value, axis, [(source, source + steps) for source in range(initial, last)])


def rotated(value, steps):
    count = lax.axis_size("feat")
    steps = steps % count
    if steps == 0:
        return value
    return lax.ppermute(value, "feat", [(s, (s + steps) % count) for s in range(count)])


def adam_update(weight, moments, grad):
    first = beta_one * moments[0] + (1.0 - beta_one) * grad
    second = beta_two * moments[1] + (1.0 - beta_two) * grad * grad
    scaled_first = first / (1.0 - beta_one**step_count)
    scaled_second = second / (1.0 - beta_two**step_count)
    updated = weight - learn_rate * scaled_first / (jnp.sqrt(scaled_second) + adam_eps)
    return (updated, jnp.stack([first, second]))


def slab_of(value, steps, width):
    count = lax.axis_size("feat")
    place = lax.rem(lax.axis_index("feat") + steps, count) * width
    return lax.dynamic_slice_in_dim(value, place, width, axis=value.ndim - 1)


def in_order(slabs):
    count = len(slabs)
    width = slabs[0].shape[-1]
    full = jnp.zeros(slabs[0].shape[:-1] + (count * width,), slabs[0].dtype)
    for steps, slab in enumerate(slabs):
        place = lax.rem(lax.axis_index("feat") + steps, count) * width
        full = lax.dynamic_update_slice_in_dim(full, slab, place, axis=full.ndim - 1)
    return full


def local(
    inputs,
    targets,
    enc_weight,
    enc_bias,
    dec_weight,
    dec_bias,
    enc_moments,
    enc_bias_moments,
    dec_moments,
    dec_bias_moments,
    block_lists,
    block_counts,
    slot_block,
):
    inputs_local = inputs[0].astype(jnp.float32)
    targets_local = targets[0].astype(jnp.float32)
    enc_local = enc_weight[0]
    encb_local = enc_bias[0]
    dec_local = dec_weight[0]
    decb_local = dec_bias[0]
    reach_count = dec_local.shape[0]
    width, row_count = inputs_local.shape
    feats = enc_local.shape[0]
    count = lax.axis_size("feat")
    tile_count = block_counts.shape[1]
    tile_rows = row_count // tile_count
    live = jnp.arange(block_lists.shape[2])[None, :] < block_counts[0][:, None]
    hits = (block_lists[0] == slot_block[0]) & live
    tile_active = jnp.any(hits, axis=1).astype(jnp.float32)
    row_mask = jnp.repeat(tile_active, tile_rows, axis=0)[None, :]

    enc_cols = jnp.concatenate(
        [rotated(slab_of(enc_local, j, width), j) for j in range(count)], axis=0
    )
    dec_cols = jnp.concatenate(
        [rotated(slab_of(dec_local, j, width), j) for j in range(count)], axis=1
    )
    partial = jnp.dot(
        enc_cols, inputs_local, precision=highest, preferred_element_type=jnp.float32
    ).reshape(count, feats, row_count)
    pre = encb_local[:, None] + sum(rotated(partial[j], -j) for j in range(count))
    codes = jnp.maximum(pre, 0.0) * row_mask
    own = jnp.concatenate([rotated(codes, j) for j in range(count)], axis=0)
    sources = jnp.stack([own] + [shifted(own, "layer", k) for k in range(1, reach_count)])
    recon = jnp.einsum("kfd,kfr->dr", dec_cols, sources, precision=high) + decb_local[:, None]
    resid = recon - targets_local
    code_parts = jnp.einsum("kfd,dr->kfr", dec_cols, resid, precision=high)
    grad_dec_cols = jnp.einsum("kfr,dr->kfd", sources, resid, precision=high)
    code_sum = code_parts[0]
    for k in range(1, reach_count):
        code_sum = code_sum + shifted(code_parts[k], "layer", -k)
    code_sum = code_sum.reshape(count, feats, row_count)
    code_grad = sum(rotated(code_sum[j], -j) for j in range(count))
    pre_grad = code_grad * row_mask * (pre > 0.0).astype(jnp.float32)
    pre_grads = jnp.concatenate([rotated(pre_grad, j) for j in range(count)], axis=0)
    grad_enc_cols = jnp.einsum("fr,dr->fd", pre_grads, inputs_local, precision=high)
    grad_enc_cols = grad_enc_cols.reshape(count, feats, width)
    grad_dec_cols = grad_dec_cols.reshape(reach_count, count, feats, width)
    grad_dec = in_order([rotated(grad_dec_cols[:, j], -j) for j in range(count)])
    grad_enc = in_order([rotated(grad_enc_cols[j], -j) for j in range(count)])
    grad_dec_bias = jnp.sum(resid, axis=1)
    grad_enc_bias = jnp.sum(pre_grad, axis=1)
    enc_new, enc_mom = adam_update(enc_local, enc_moments[:, 0], grad_enc)
    encb_new, encb_mom = adam_update(encb_local, enc_bias_moments[:, 0], grad_enc_bias)
    dec_new, dec_mom = adam_update(dec_local, dec_moments[:, 0], grad_dec)
    decb_new, decb_mom = adam_update(decb_local, dec_bias_moments[:, 0], grad_dec_bias)
    return (
        enc_new[None],
        encb_new[None],
        dec_new[None],
        decb_new[None],
        enc_mom[:, None],
        encb_mom[:, None],
        dec_mom[:, None],
        decb_mom[:, None],
    )


def solution(mesh):
    cols = P(("group", "layer"), "feat", None)
    vec = P(("group", "layer"), "feat")
    dec = P(("group", "layer"), None, "feat", None)
    cols_mom = P(None, ("group", "layer"), "feat", None)
    vec_mom = P(None, ("group", "layer"), "feat")
    dec_mom = P(None, ("group", "layer"), None, "feat", None)
    return jax.shard_map(
        local,
        mesh=mesh,
        in_specs=(
            cols,
            cols,
            cols,
            vec,
            dec,
            vec,
            cols_mom,
            vec_mom,
            dec_mom,
            vec_mom,
            P(("group", "layer"), None, None),
            P(("group", "layer"), None),
            P(("group", "layer")),
        ),
        out_specs=(cols, vec, dec, vec, cols_mom, vec_mom, dec_mom, vec_mom),
        check_vma=False,
    )
```

```python
import functools

import jax
import jax.numpy as jnp
from jax import lax
from jax.experimental import pallas as pl
from jax.experimental.pallas import tpu as pltpu
from jax.sharding import PartitionSpec as P

beta_one = 0.9
beta_two = 0.999
learn_rate = 0.001
adam_eps = 1e-08
step_count = 100.0
highest = lax.Precision.HIGHEST
lanes = 128
log_two = 0.6931471805599453
levels = 32767.0
vmem_bytes = 60 * 1024 * 1024
held_types = (jnp.float32, jnp.bfloat16, jnp.int16)


def shifted(value, axis, steps):
    count = lax.axis_size(axis)
    initial, last = (max(0, -steps), min(count, count - steps))
    return lax.ppermute(value, axis, [(source, source + steps) for source in range(initial, last)])


def rotated(value, steps, first_layer=0):
    count = lax.axis_size("feat")
    steps = steps % count
    if steps == 0:
        return value
    pairs = [
        (layer * count + s, layer * count + (s + steps) % count)
        for layer in range(first_layer, lax.axis_size("layer"))
        for s in range(count)
    ]
    return lax.ppermute(value, ("layer", "feat"), pairs)


def adam_update(weight, moments, grad):
    first = beta_one * moments[0] + (1.0 - beta_one) * grad
    second = beta_two * moments[1] + (1.0 - beta_two) * grad * grad
    scaled_first = first / (1.0 - beta_one**step_count)
    scaled_second = second / (1.0 - beta_two**step_count)
    updated = weight - learn_rate * scaled_first / (jnp.sqrt(scaled_second) + adam_eps)
    return (updated, jnp.stack([first, second]))


def slab_of(value, steps, width):
    count = lax.axis_size("feat")
    place = lax.rem(lax.axis_index("feat") + steps, count) * width
    return lax.dynamic_slice_in_dim(value, place, width, axis=value.ndim - 1)


def code_into(out_ref, rows, value):
    width = value.shape[1]
    top = jnp.max(jnp.abs(value), axis=1, keepdims=True)
    exponent = jnp.ceil(jnp.log(jnp.maximum(top, 1e-30)) * (8.0 / log_two))
    scale = levels * jnp.exp(exponent * (-log_two / 8.0))
    whole = jnp.clip(jnp.round(value * scale), -levels, levels)
    out_ref[rows, 0:width] = whole.astype(jnp.int32).astype(jnp.int16)
    tail = jnp.broadcast_to(exponent, (value.shape[0], lanes))
    out_ref[rows, width : width + lanes] = tail.astype(jnp.int32).astype(jnp.int16)


def step_of(exponent):
    return jnp.exp(exponent.astype(jnp.float32) * (log_two / 8.0)) * (1.0 / levels)


def decoded(ref, rows):
    width = ref.shape[1] - lanes
    whole = ref[rows, 0:width].astype(jnp.int32).astype(jnp.float32)
    exponent = ref[rows, width : width + lanes].astype(jnp.int32)[:, 0:1]
    return whole * step_of(exponent)


def split(value):
    upper = value.astype(jnp.bfloat16)
    return upper, (value - upper.astype(jnp.float32)).astype(jnp.bfloat16)


def product(left, right, dims):
    dot = functools.partial(
        lax.dot_general, dimension_numbers=(dims, ((), ())), preferred_element_type=jnp.float32
    )
    return dot(left[0], right[0]) + (dot(left[0], right[1]) + dot(left[1], right[0]))


def blocks_of(size, block):
    block = min(size, block)
    return [slice(start, start + block) for start in range(0, size, block)]


def held_bytes(array):
    size = array.dtype.itemsize
    if len(array.shape) == 1:
        return 4096
    rows, columns = array.shape[-2:]
    tile = 32 // size
    rows, columns = -(-rows // tile) * tile, -(-columns // lanes) * lanes
    for extent in array.shape[:-2]:
        rows = rows * extent
    return rows * columns * size


def call(kernel, out_shape, args, flops=0, scratch=(), after=(), far=(), far_out=()):
    size = sum(a.size * a.dtype.itemsize for a in [*far, *args])
    size += sum(o.size * o.dtype.itemsize for o in [*far_out, *out_shape])
    distant, taken, skipped = len(far), len(args), len(after)
    need = sum(held_bytes(a) for a in [*args, *out_shape]) + 4 * 1024 * 1024
    need += sum(held_bytes(a) for a in scratch if a.dtype in held_types)

    def body(*refs):
        kernel(*refs[: distant + taken], *refs[distant + taken + skipped :])

    spaces = [pltpu.HBM] * distant
    spaces += [pltpu.SMEM if a.shape == (1,) else pltpu.VMEM for a in args]
    spaces += [pl.ANY] * skipped
    out_spaces = [pltpu.HBM] * len(far_out) + [pltpu.VMEM] * len(out_shape)
    return pl.pallas_call(
        body,
        out_shape=(*far_out, *out_shape),
        in_specs=[pl.BlockSpec(memory_space=space) for space in spaces],
        out_specs=tuple(pl.BlockSpec(memory_space=space) for space in out_spaces),
        scratch_shapes=list(scratch),
        cost_estimate=pl.CostEstimate(flops=flops, bytes_accessed=size, transcendentals=0),
        compiler_params=pltpu.CompilerParams(vmem_limit_bytes=max(need, vmem_bytes if far else 0)),
    )(*far, *args, *after)


def buffer_like(array):
    return pltpu.VMEM(array.shape, array.dtype)


class Fetched:
    def __init__(self, sources, buffers, semaphores):
        self.copies = [
            pltpu.make_async_copy(source, held, semaphores.at[i])
            for i, (source, held) in enumerate(zip(sources, buffers, strict=True))
        ]
        self.buffers = buffers
        for copy in self.copies:
            copy.start()

    def __getitem__(self, i):
        self.copies[i].wait()
        return self.buffers[i]


def shape(rows, columns, dtype=jnp.float32):
    return jax.ShapeDtypeStruct((rows, columns), dtype)


def coded_shape(rows, columns):
    return jax.ShapeDtypeStruct((rows, columns + lanes), jnp.int16)


def pack_kernel(count, first, last, me_ref, in_ref, *outs):
    reach, feats, total = in_ref.shape
    width = total // count
    for j in range(count):
        place = pl.multiple_of(lax.rem(me_ref[0] + j, count) * width, lanes)
        for k in range(first, last):
            rows = slice((k - first) * feats, (k - first + 1) * feats)
            code_into(outs[j], rows, in_ref[k, :, pl.ds(place, width)])


def packed(me, weights, first, last, after=()):
    count = lax.axis_size("feat")
    reach, feats, total = weights.shape
    out = coded_shape((last - first) * feats, total // count)
    kernel = functools.partial(pack_kernel, count, first, last)
    return call(kernel, [out] * count, [me, weights], after=after)


def adam_kernel(count, starts, me_ref, *refs):
    grads, (weight_ref, moments_ref, new_ref, new_moments_ref) = refs[:-4], refs[-4:]
    k = pl.program_id(0)
    feats, total = weight_ref.shape[1:]
    width = total // count

    def update(j, grad):
        place = pl.multiple_of(lax.rem(me_ref[0] + j, count) * width, lanes)
        cols = pl.ds(place, width)
        first = beta_one * moments_ref[0, 0, :, cols] + (1.0 - beta_one) * grad
        second = beta_two * moments_ref[1, 0, :, cols] + (1.0 - beta_two) * grad * grad
        new_moments_ref[0, 0, :, cols] = first
        new_moments_ref[1, 0, :, cols] = second
        scaled_first = first * (learn_rate / (1.0 - beta_one**step_count))
        scaled_second = second * (1.0 / (1.0 - beta_two**step_count))
        new_ref[0, :, cols] = weight_ref[0, :, cols] - scaled_first / (
            jnp.sqrt(scaled_second) + adam_eps
        )

    for part, (start, stop) in enumerate(starts):

        @pl.when((k >= start) & (k < stop))
        def _(part=part):
            for j in range(count):
                update(j, decoded(grads[part * count + j], slice(None)))


def adam_call(me, starts, grads, weight, moments, after=()):
    count = lax.axis_size("feat")
    reach, feats, total = weight.shape
    skipped = len(after)

    def body(*refs):
        adam_kernel(count, starts, *refs[: len(grads) + 3], *refs[len(grads) + 3 + skipped :])

    def grad_spec(start, stop):
        coded_width = total // count + lanes
        return pl.BlockSpec(
            (feats, coded_width), lambda k: (jnp.clip(k - start, 0, stop - start - 1), 0)
        )

    weight_spec = pl.BlockSpec((1, feats, total), lambda k: (k, 0, 0))
    moments_spec = pl.BlockSpec((2, 1, feats, total), lambda k: (0, k, 0, 0))
    return pl.pallas_call(
        body,
        grid=(reach,),
        out_shape=(
            jax.ShapeDtypeStruct(weight.shape, weight.dtype),
            jax.ShapeDtypeStruct(moments.shape, moments.dtype),
        ),
        in_specs=[pl.BlockSpec(memory_space=pltpu.SMEM)]
        + [grad_spec(*limits) for limits in starts for _ in range(count)]
        + [weight_spec, moments_spec]
        + [pl.BlockSpec(memory_space=pl.ANY)] * skipped,
        out_specs=(weight_spec, moments_spec),
        cost_estimate=pl.CostEstimate(
            flops=20 * weight.size, bytes_accessed=26 * weight.size, transcendentals=weight.size
        ),
        compiler_params=pltpu.CompilerParams(vmem_limit_bytes=24 * 1024 * 1024),
    )(me, *grads, weight, moments, *after)


def gather_kernel(*refs):
    *parts, out_ref = refs
    feats = parts[0].shape[0]
    for j, part in enumerate(parts):
        out_ref[j * feats : (j + 1) * feats, :] = part[...]


def codes_kernel(count, *refs):
    parts, bias_ref, mask_ref, codes_ref, coded_ref = refs[:count], *refs[count:]
    pre = bias_ref[...] + sum(part[...] for part in parts)
    codes = jnp.maximum(pre, 0.0) * mask_ref[...]
    codes_ref[...] = codes
    code_into(coded_ref, slice(None), codes)


def resid_kernel(count, reach, feats, starts, *refs):
    parts = len(starts)
    sources = parts * count + count + reach - 1 + 2
    fars, refs = refs[:sources], refs[sources:]
    res_out, src_out, refs = refs[0:2], refs[2:4], refs[4:]
    part_ref, refs = refs[0], refs[1:]
    coded_parts, refs = refs[: reach - 1], refs[reach - 1 :]
    sum_ref, refs = refs[0], refs[1:]
    buffers, refs = refs[:sources], refs[sources:]
    w_full, s_full, w_up, w_low, res_up, res_low, src_up, src_low, arrive, leave = refs
    held = Fetched(fars, buffers, arrive)
    block = count * feats
    owns, moves = parts * count, parts * count + count
    near = [held[owns + j] for j in range(count)]
    for j in range(count):
        s_full[j * feats : (j + 1) * feats, :] = decoded(near[j], slice(None))
    for part, (start, stop) in enumerate(starts):
        for j in range(count):
            weights = held[part * count + j]
            for k in range(start, stop):
                rows = slice(k * block + j * feats, k * block + (j + 1) * feats)
                w_full[rows, :] = decoded(weights, slice((k - start) * feats, (k - start + 1) * feats))
    for k in range(1, reach):
        moved = held[moves + k - 1]
        for rows in blocks_of(block, 32):
            s_full[k * block + rows.start : k * block + rows.stop, :] = decoded(moved, rows)
    for rows in blocks_of(reach * block, 32):
        w_up[rows, :], w_low[rows, :] = split(w_full[rows, :])
        src_up[rows, :], src_low[rows, :] = split(s_full[rows, :])
    sends = [
        pltpu.make_async_copy(source, out, leave.at[i])
        for i, (source, out) in enumerate(zip((src_up, src_low), src_out))
    ]
    targets_ref, bias_ref = held[sources - 2], held[sources - 1]
    for send in sends:
        send.start()
    width, row_count = targets_ref.shape
    chunk = min(256, width)

    def recon_chunk(i, carry):
        cols = pl.ds(pl.multiple_of(i * chunk, chunk), chunk)
        recon = product(
            (w_up[:, cols], w_low[:, cols]), (src_up[...], src_low[...]), ((0,), (0,))
        )
        resid = recon + bias_ref[cols, :] - targets_ref[cols, :].astype(jnp.float32)
        sum_ref[cols, :] = jnp.sum(resid, axis=1, keepdims=True)
        res_up[cols, :], res_low[cols, :] = split(resid)
        return carry

    lax.fori_loop(0, width // chunk, recon_chunk, 0)
    more = [
        pltpu.make_async_copy(source, out, leave.at[2 + i])
        for i, (source, out) in enumerate(zip((res_up, res_low), res_out))
    ]
    for send in more:
        send.start()
    span = min(256, row_count)

    def part_chunk(i, carry):
        cols = pl.ds(pl.multiple_of(i * span, span), span)
        s_full[:, cols] = product(
            (w_up[...], w_low[...]), (res_up[:, cols], res_low[:, cols]), ((1,), (0,))
        )
        return carry

    lax.fori_loop(0, row_count // span, part_chunk, 0)
    part_ref[...] = s_full[0:block, :]
    for k in range(1, reach):
        for rows in blocks_of(block, 32):
            source = slice(k * block + rows.start, k * block + rows.stop)
            code_into(coded_parts[k - 1], rows, s_full[source, :])
    for send in [*sends, *more]:
        send.wait()


def grad_dec_kernel(count, feats, starts, *refs):
    src_far, res_far, refs = refs[0:2], refs[2:4], refs[4:]
    outs, refs = refs[: len(starts) * count], refs[len(starts) * count :]
    src_up, src_low, res_up, res_low, grad, arrive = refs
    width = res_up.shape[0]
    chunk = min(256, width)
    held = Fetched(
        [*src_far] + [far.at[pl.ds(i, chunk)] for i in range(0, width, chunk) for far in res_far],
        [src_up, src_low]
        + [ref.at[pl.ds(i, chunk)] for i in range(0, width, chunk) for ref in (res_up, res_low)],
        arrive,
    )
    source = (held[0][...], held[1][...])
    for i in range(width // chunk):
        right = (held[2 + 2 * i][...], held[3 + 2 * i][...])
        grad[:, i * chunk : (i + 1) * chunk] = product(source, right, ((1,), (1,)))
    for part, (start, stop) in enumerate(starts):
        for j in range(count):
            for k in range(start, stop):
                row = (k * count + j) * feats
                rows = slice((k - start) * feats, (k - start + 1) * feats)
                code_into(outs[part * count + j], rows, grad[row : row + feats, :])


def code_sum_kernel(count, feats, moved_count, *refs):
    own, moved, outs = refs[0], refs[1 : 1 + moved_count], refs[1 + moved_count :]
    for j in range(count):
        rows = slice(j * feats, (j + 1) * feats)
        total = own[rows, :]
        for ref in moved:
            total = total + decoded(ref, rows)
        if j == 0:
            outs[0][...] = total
        else:
            code_into(outs[j], slice(None), total)


def pre_grad_kernel(count, *refs):
    own, arrived, codes_ref, coded_ref, sum_ref = refs[0], refs[1:count], *refs[count:]
    total = own[...]
    for ref in arrived:
        total = total + decoded(ref, slice(None))
    pre_grad = jnp.where(codes_ref[...] > 0.0, total, 0.0)
    sum_ref[...] = jnp.sum(pre_grad, axis=1, keepdims=True)
    code_into(coded_ref, slice(None), pre_grad)


def grad_enc_kernel(count, feats, *refs):
    grads, inputs_ref, outs, full, grad = refs[:count], refs[count], *[refs[count + 1 : -2]], *refs[-2:]
    for j in range(count):
        full[j * feats : (j + 1) * feats, :] = decoded(grads[j], slice(None))
    upper, lower = split(full[...])
    width = inputs_ref.shape[0]
    chunk = min(256, width)
    dot = functools.partial(
        lax.dot_general,
        dimension_numbers=(((1,), (1,)), ((), ())),
        preferred_element_type=jnp.float32,
    )
    for rows in blocks_of(width, chunk):
        right = inputs_ref[rows, :]
        grad[:, rows] = dot(upper, right) + dot(lower, right)
    for j in range(count):
        code_into(outs[j], slice(None), grad[j * feats : (j + 1) * feats, :])


def local(
    inputs,
    targets,
    enc_weight,
    enc_bias,
    dec_weight,
    dec_bias,
    enc_moments,
    enc_bias_moments,
    dec_moments,
    dec_bias_moments,
    block_lists,
    block_counts,
    slot_block,
):
    inputs_local = inputs[0]
    targets_local = targets[0]
    enc_local = enc_weight[0]
    encb_local = enc_bias[0]
    dec_local = dec_weight[0]
    decb_local = dec_bias[0]
    reach = dec_local.shape[0]
    width, row_count = inputs_local.shape
    feats = enc_local.shape[0]
    count = lax.axis_size("feat")
    block = count * feats
    depth = reach * block
    tile_count = block_counts.shape[1]
    tile_rows = row_count // tile_count
    live = jnp.arange(block_lists.shape[2])[None, :] < block_counts[0][:, None]
    hits = (block_lists[0] == slot_block[0]) & live
    tile_active = jnp.any(hits, axis=1).astype(jnp.float32)
    row_mask = jnp.repeat(tile_active, tile_rows, axis=0)[None, :]

    enc_cols = jnp.concatenate(
        [rotated(slab_of(enc_local, j, width), j) for j in range(count)], axis=0
    )
    me = lax.axis_index("feat").astype(jnp.int32).reshape(1)
    starts = ((0, reach - 1), (reach - 1, reach)) if reach > 1 else ((0, reach),)
    dec_cols = []
    for first, last in starts[1:]:
        sent = packed(me, dec_local, first, last)
        dec_cols += [rotated(sent[j], j, first) for j in range(count)]
    partial = jnp.dot(
        enc_cols,
        inputs_local.astype(jnp.float32),
        precision=highest,
        preferred_element_type=jnp.float32,
    ).reshape(count, feats, row_count)
    partials = [rotated(partial[j], -j) for j in range(count)]
    codes, coded_codes = call(
        functools.partial(codes_kernel, count),
        [shape(feats, row_count), coded_shape(feats, row_count)],
        [*partials, encb_local[:, None], row_mask],
        after=dec_cols[1:count],
    )
    own = [rotated(coded_codes, j) for j in range(count)]
    gathered = call(gather_kernel, [coded_shape(block, row_count)], own)[0]
    moved = [shifted(gathered, "layer", k) for k in range(1, reach)]
    sent = packed(me, dec_local, *starts[0], after=[coded_codes])
    dec_cols = [rotated(sent[j], j) for j in range(count)] + dec_cols
    half = jnp.bfloat16
    far = [*dec_cols, *own, *moved, targets_local, decb_local[:, None]]
    outs = call(
        functools.partial(resid_kernel, count, reach, feats, starts),
        [shape(block, row_count)]
        + [coded_shape(block, row_count)] * (reach - 1)
        + [shape(width, 1)],
        [],
        flops=12 * depth * width * row_count,
        scratch=[buffer_like(a) for a in far]
        + [pltpu.VMEM((depth, width), jnp.float32), pltpu.VMEM((depth, row_count), jnp.float32)]
        + [pltpu.VMEM((depth, width), half)] * 2
        + [pltpu.VMEM((width, row_count), half)] * 2
        + [pltpu.VMEM((depth, row_count), half)] * 2
        + [pltpu.SemaphoreType.DMA((len(far),)), pltpu.SemaphoreType.DMA((4,))],
        far=far,
        far_out=[shape(width, row_count, half)] * 2 + [shape(depth, row_count, half)] * 2,
    )
    res, src, part, parts, grad_dec_bias = outs[0:2], outs[2:4], outs[4], outs[5:-1], outs[-1]
    returned = [shifted(parts[k - 1], "layer", -k) for k in range(1, reach)]

    grad_parts = call(
        functools.partial(grad_dec_kernel, count, feats, starts),
        [coded_shape((last - first) * feats, width) for first, last in starts for _ in range(count)],
        [],
        flops=6 * depth * width * row_count,
        scratch=[pltpu.VMEM((depth, row_count), half)] * 2
        + [pltpu.VMEM((width, row_count), half)] * 2
        + [pltpu.VMEM((depth, width), jnp.float32)]
        + [pltpu.SemaphoreType.DMA((2 + 2 * (width // min(256, width)),))],
        far=[*src, *res],
    )
    grad_dec_cols = [
        rotated(grad_parts[part * count + j], -j, first if part else 0)
        for part, (first, last) in enumerate(starts)
        for j in range(count)
    ]
    sums = call(
        functools.partial(code_sum_kernel, count, feats, reach - 1),
        [shape(feats, row_count)] + [coded_shape(feats, row_count)] * (count - 1),
        [part, *returned],
        after=[grad_parts[0]],
    )
    arrived = [rotated(sums[j], -j) for j in range(count)]
    coded_grad, grad_enc_bias = call(
        functools.partial(pre_grad_kernel, count),
        [coded_shape(feats, row_count), shape(feats, 1)],
        [*arrived, codes],
        after=grad_dec_cols[1:count],
    )
    pre_grads = [rotated(coded_grad, j) for j in range(count)]
    grad_enc_cols = call(
        functools.partial(grad_enc_kernel, count, feats),
        [coded_shape(feats, width)] * count,
        [*pre_grads, inputs_local],
        flops=4 * block * width * row_count,
        scratch=[
            pltpu.VMEM((block, row_count), jnp.float32),
            pltpu.VMEM((block, width), jnp.float32),
        ],
    )
    dec_new, dec_mom = adam_call(
        me, starts, grad_dec_cols, dec_local, dec_moments[:, 0], after=[grad_enc_cols[0]]
    )
    enc_arrived = [rotated(grad_enc_cols[j], -j) for j in range(count)]
    enc_new, enc_mom = adam_call(me, ((0, 1),), enc_arrived, enc_local[None], enc_moments)
    encb_new, encb_mom = adam_update(encb_local, enc_bias_moments[:, 0], grad_enc_bias[:, 0])
    decb_new, decb_mom = adam_update(decb_local, dec_bias_moments[:, 0], grad_dec_bias[:, 0])
    return (
        enc_new,
        encb_new[None],
        dec_new[None],
        decb_new[None],
        enc_mom,
        encb_mom[:, None],
        dec_mom[:, None],
        decb_mom[:, None],
    )


def solution(mesh):
    cols = P(("group", "layer"), "feat", None)
    vec = P(("group", "layer"), "feat")
    dec = P(("group", "layer"), None, "feat", None)
    cols_mom = P(None, ("group", "layer"), "feat", None)
    vec_mom = P(None, ("group", "layer"), "feat")
    dec_mom = P(None, ("group", "layer"), None, "feat", None)
    return jax.shard_map(
        local,
        mesh=mesh,
        in_specs=(
            cols,
            cols,
            cols,
            vec,
            dec,
            vec,
            cols_mom,
            vec_mom,
            dec_mom,
            vec_mom,
            P(("group", "layer"), None, None),
            P(("group", "layer"), None),
            P(("group", "layer")),
        ),
        out_specs=(cols, vec, dec, vec, cols_mom, vec_mom, dec_mom, vec_mom),
        check_vma=False,
    )
```

```python
import functools

import jax
import jax.numpy as jnp
from jax import lax
from jax.experimental import pallas as pl
from jax.experimental.pallas import tpu as pltpu
from jax.sharding import PartitionSpec as P

beta_one = 0.9
beta_two = 0.999
learn_rate = 0.001
adam_eps = 1e-08
step_count = 100.0
highest = lax.Precision.HIGHEST
lanes = 128
log_two = 0.6931471805599453
levels = 32767.0
vmem_bytes = 60 * 1024 * 1024
held_types = (jnp.float32, jnp.bfloat16, jnp.int16)


def shifted(value, axis, steps):
    count = lax.axis_size(axis)
    initial, last = (max(0, -steps), min(count, count - steps))
    return lax.ppermute(value, axis, [(source, source + steps) for source in range(initial, last)])


def rotated(value, steps, first_layer=0):
    count = lax.axis_size("feat")
    steps = steps % count
    if steps == 0:
        return value
    pairs = [
        (layer * count + s, layer * count + (s + steps) % count)
        for layer in range(first_layer, lax.axis_size("layer"))
        for s in range(count)
    ]
    return lax.ppermute(value, ("layer", "feat"), pairs)


def adam_update(weight, moments, grad):
    first = beta_one * moments[0] + (1.0 - beta_one) * grad
    second = beta_two * moments[1] + (1.0 - beta_two) * grad * grad
    scaled_first = first / (1.0 - beta_one**step_count)
    scaled_second = second / (1.0 - beta_two**step_count)
    updated = weight - learn_rate * scaled_first / (jnp.sqrt(scaled_second) + adam_eps)
    return (updated, jnp.stack([first, second]))


def slab_of(value, steps, width):
    count = lax.axis_size("feat")
    place = lax.rem(lax.axis_index("feat") + steps, count) * width
    return lax.dynamic_slice_in_dim(value, place, width, axis=value.ndim - 1)


exponent_bits = 12
exponent_offset = 1024


def lane_index(rows):
    return lax.broadcasted_iota(jnp.int32, (rows, lanes), 1)


def code_into(out_ref, rows, value):
    count, width = value.shape
    top = jnp.max(jnp.abs(value), axis=1, keepdims=True)
    exponent = jnp.ceil(jnp.log(jnp.maximum(top, 1e-30)) * (8.0 / log_two))
    scale = levels * jnp.exp(exponent * (-log_two / 8.0))
    whole = jnp.clip(jnp.round(value * scale), -levels, levels).astype(jnp.int32)
    lane = lane_index(count)
    shown = jnp.broadcast_to(exponent.astype(jnp.int32) + exponent_offset, (count, lanes))
    bits = lax.shift_right_logical(shown, jnp.minimum(lane, exponent_bits)) & 1
    first = whole[:, 0:lanes]
    first = jnp.where(lane < exponent_bits, (first & -2) | bits, first)
    out_ref[rows, 0:lanes] = first.astype(jnp.int16)
    if width > lanes:
        out_ref[rows, lanes:width] = whole[:, lanes:width].astype(jnp.int16)


def decoded(ref, rows):
    whole = ref[rows, :].astype(jnp.int32)
    count = whole.shape[0]
    lane = lane_index(count)
    bits = lax.shift_left(whole[:, 0:lanes] & 1, jnp.minimum(lane, exponent_bits))
    bits = jnp.where(lane < exponent_bits, bits, 0).astype(jnp.float32)
    exponent = jnp.sum(bits, axis=1, keepdims=True) - exponent_offset
    step = jnp.exp(jnp.maximum(exponent, -880.0) * (log_two / 8.0)) * (1.0 / levels)
    return whole.astype(jnp.float32) * step


def split(value):
    upper = value.astype(jnp.bfloat16)
    return upper, (value - upper.astype(jnp.float32)).astype(jnp.bfloat16)


def product(left, right, dims):
    dot = functools.partial(
        lax.dot_general, dimension_numbers=(dims, ((), ())), preferred_element_type=jnp.float32
    )
    return dot(left[0], right[0]) + (dot(left[0], right[1]) + dot(left[1], right[0]))


def blocks_of(size, block):
    block = min(size, block)
    return [slice(start, start + block) for start in range(0, size, block)]


def held_bytes(array):
    size = array.dtype.itemsize
    if len(array.shape) == 1:
        return 4096
    rows, columns = array.shape[-2:]
    tile = 32 // size
    rows, columns = -(-rows // tile) * tile, -(-columns // lanes) * lanes
    for extent in array.shape[:-2]:
        rows = rows * extent
    return rows * columns * size


def call(kernel, out_shape, args, flops=0, scratch=(), after=(), far=(), far_out=(), alone=True):
    size = sum(a.size * a.dtype.itemsize for a in [*far, *args])
    size += sum(o.size * o.dtype.itemsize for o in [*far_out, *out_shape])
    distant, taken, skipped = len(far), len(args), len(after)
    need = sum(held_bytes(a) for a in [*args, *out_shape]) + 4 * 1024 * 1024
    need += sum(held_bytes(a) for a in scratch if a.dtype in held_types)

    def body(*refs):
        kernel(*refs[: distant + taken], *refs[distant + taken + skipped :])

    spaces = [pltpu.HBM] * distant
    spaces += [pltpu.SMEM if a.shape == (1,) else pltpu.VMEM for a in args]
    spaces += [pl.ANY] * skipped
    out_spaces = [pltpu.HBM] * len(far_out) + [pltpu.VMEM] * len(out_shape)
    return pl.pallas_call(
        body,
        out_shape=(*far_out, *out_shape),
        in_specs=[pl.BlockSpec(memory_space=space) for space in spaces],
        out_specs=tuple(pl.BlockSpec(memory_space=space) for space in out_spaces),
        scratch_shapes=list(scratch),
        cost_estimate=pl.CostEstimate(flops=flops, bytes_accessed=size, transcendentals=0),
        compiler_params=pltpu.CompilerParams(vmem_limit_bytes=max(need, vmem_bytes if far and alone else 0)),
    )(*far, *args, *after)


def buffer_like(array):
    return pltpu.VMEM(array.shape, array.dtype)


class Fetched:
    def __init__(self, sources, buffers, semaphores):
        self.copies = [
            pltpu.make_async_copy(source, held, semaphores.at[i])
            for i, (source, held) in enumerate(zip(sources, buffers, strict=True))
        ]
        self.buffers = buffers
        for copy in self.copies:
            copy.start()

    def __getitem__(self, i):
        self.copies[i].wait()
        return self.buffers[i]


def shape(rows, columns, dtype=jnp.float32):
    return jax.ShapeDtypeStruct((rows, columns), dtype)


def coded_shape(rows, columns):
    return jax.ShapeDtypeStruct((rows, columns), jnp.int16)


def pack_kernel(count, first, last, me_ref, in_ref, *outs):
    reach, feats, total = in_ref.shape
    width = total // count
    for j in range(count):
        place = pl.multiple_of(lax.rem(me_ref[0] + j, count) * width, lanes)
        for k in range(first, last):
            rows = slice((k - first) * feats, (k - first + 1) * feats)
            code_into(outs[j], rows, in_ref[k, :, pl.ds(place, width)])


def packed(me, weights, first, last, after=()):
    count = lax.axis_size("feat")
    reach, feats, total = weights.shape
    out = coded_shape((last - first) * feats, total // count)
    kernel = functools.partial(pack_kernel, count, first, last)
    return call(kernel, [out] * count, [me, weights], after=after)


def adam_kernel(count, me_ref, *refs):
    grads, (weight_ref, moments_ref), (new_ref, new_moments_ref) = refs[:count], refs[count : count + 2], refs[-2:]
    width = weight_ref.shape[2] // count
    for j in range(count):
        place = pl.multiple_of(lax.rem(me_ref[0] + j, count) * width, lanes)
        cols = pl.ds(place, width)
        grad = decoded(grads[j], slice(None))
        first = beta_one * moments_ref[0, 0, :, cols] + (1.0 - beta_one) * grad
        second = beta_two * moments_ref[1, 0, :, cols] + (1.0 - beta_two) * grad * grad
        new_moments_ref[0, 0, :, cols] = first
        new_moments_ref[1, 0, :, cols] = second
        scaled_first = first * (learn_rate / (1.0 - beta_one**step_count))
        scaled_second = second * (1.0 / (1.0 - beta_two**step_count))
        new_ref[0, :, cols] = weight_ref[0, :, cols] - scaled_first / (
            jnp.sqrt(scaled_second) + adam_eps
        )


def adam_call(me, start, stop, grads, weight, moments, filled=(), after=()):
    count = lax.axis_size("feat")
    feats, total = weight.shape[1:]
    grad_spec = pl.BlockSpec((feats, total // count), lambda k: (k, 0))
    weight_spec = pl.BlockSpec((1, feats, total), lambda k: (start + k, 0, 0))
    moments_spec = pl.BlockSpec((2, 1, feats, total), lambda k: (0, start + k, 0, 0))
    place = 1 + count + 2
    return pl.pallas_call(
        functools.partial(adam_kernel, count),
        grid=(stop - start,),
        out_shape=(
            jax.ShapeDtypeStruct(weight.shape, weight.dtype),
            jax.ShapeDtypeStruct(moments.shape, moments.dtype),
        ),
        in_specs=[pl.BlockSpec(memory_space=pltpu.SMEM)]
        + [grad_spec] * count
        + [weight_spec, moments_spec]
        + [pl.BlockSpec(memory_space=pl.ANY)] * (len(filled) + len(after)),
        out_specs=(weight_spec, moments_spec),
        input_output_aliases={place + i: i for i in range(len(filled))},
        cost_estimate=pl.CostEstimate(
            flops=20 * (stop - start) * feats * total,
            bytes_accessed=26 * (stop - start) * feats * total,
            transcendentals=(stop - start) * feats * total,
        ),
        compiler_params=pltpu.CompilerParams(vmem_limit_bytes=24 * 1024 * 1024),
    )(me, *grads, weight, moments, *filled, *after)


def gather_kernel(*refs):
    *parts, out_ref = refs
    feats = parts[0].shape[0]
    for j, part in enumerate(parts):
        out_ref[j * feats : (j + 1) * feats, :] = part[...]


def codes_kernel(count, *refs):
    parts, bias_ref, mask_ref, codes_ref, coded_ref = refs[:count], *refs[count:]
    pre = bias_ref[...] + sum(part[...] for part in parts)
    codes = jnp.maximum(pre, 0.0) * mask_ref[...]
    codes_ref[...] = codes
    code_into(coded_ref, slice(None), codes)


def weights_kernel(count, feats, starts, *refs):
    parts = len(starts)
    fars, up_ref, low_ref, refs = refs[: parts * count], *refs[parts * count :][:2], refs[parts * count + 2 :]
    *buffers, full, arrive = refs
    held = Fetched(fars, buffers, arrive)
    for part, (start, stop) in enumerate(starts):
        for j in range(count):
            weights = held[part * count + j]
            for k in range(start, stop):
                row = (k * count + j) * feats
                rows = slice((k - start) * feats, (k - start + 1) * feats)
                full[row : row + feats, :] = decoded(weights, rows)
    for rows in blocks_of(full.shape[0], 32):
        up_ref[rows, :], low_ref[rows, :] = split(full[rows, :])


def main_kernel(count, reach, feats, starts, *refs):
    sources, results = count + reach - 1 + 4, reach + len(starts) * count
    fars, far_outs, sum_ref = refs[:sources], refs[sources : sources + results], refs[sources + results]
    refs = refs[sources + results + 1 :]
    buffers, outs, refs = refs[:sources], refs[sources : sources + results], refs[sources + results :]
    full, grad, res_up, res_low, src_up, src_low, arrive, leave = refs
    held = Fetched(fars, buffers, arrive)
    sends = [
        pltpu.make_async_copy(source, out, leave.at[i])
        for i, (source, out) in enumerate(zip(outs, far_outs, strict=True))
    ]
    block = count * feats
    for j in range(count):
        full[j * feats : (j + 1) * feats, :] = decoded(held[j], slice(None))
    for k in range(1, reach):
        moved = held[count + k - 1]
        for rows in blocks_of(block, 32):
            full[k * block + rows.start : k * block + rows.stop, :] = decoded(moved, rows)
    for rows in blocks_of(reach * block, 32):
        src_up[rows, :], src_low[rows, :] = split(full[rows, :])
    w_up, w_low = held[sources - 4], held[sources - 3]
    bias_ref, targets_ref = held[sources - 2], held[sources - 1]
    width, row_count = targets_ref.shape
    for cols in blocks_of(width, 256):
        recon = product(
            (w_up[:, cols], w_low[:, cols]), (src_up[...], src_low[...]), ((0,), (0,))
        )
        resid = recon + bias_ref[cols, :] - targets_ref[cols, :].astype(jnp.float32)
        sum_ref[cols, :] = jnp.sum(resid, axis=1, keepdims=True)
        res_up[cols, :], res_low[cols, :] = split(resid)
    for cols in blocks_of(row_count, 256):
        full[:, cols] = product(
            (w_up[...], w_low[...]), (res_up[:, cols], res_low[:, cols]), ((1,), (0,))
        )
    outs[0][...] = full[0:block, :]
    sends[0].start()
    for k in range(1, reach):
        for rows in blocks_of(block, 32):
            source = slice(k * block + rows.start, k * block + rows.stop)
            code_into(outs[k], rows, full[source, :])
        sends[k].start()
    for rows in blocks_of(width, 256):
        grad[:, rows] = product(
            (src_up[...], src_low[...]), (res_up[rows, :], res_low[rows, :]), ((1,), (1,))
        )
    for part, (start, stop) in enumerate(starts):
        for j in range(count):
            place = reach + part * count + j
            for k in range(start, stop):
                row = (k * count + j) * feats
                rows = slice((k - start) * feats, (k - start + 1) * feats)
                code_into(outs[place], rows, grad[row : row + feats, :])
            sends[place].start()
    for send in sends:
        send.wait()


def code_sum_kernel(count, feats, moved_count, *refs):
    own, moved, outs = refs[0], refs[1 : 1 + moved_count], refs[1 + moved_count :]
    for j in range(count):
        rows = slice(j * feats, (j + 1) * feats)
        total = own[rows, :]
        for ref in moved:
            total = total + decoded(ref, rows)
        if j == 0:
            outs[0][...] = total
        else:
            code_into(outs[j], slice(None), total)


def pre_grad_kernel(count, *refs):
    own, arrived, codes_ref, coded_ref, sum_ref = refs[0], refs[1:count], *refs[count:]
    total = own[...]
    for ref in arrived:
        total = total + decoded(ref, slice(None))
    pre_grad = jnp.where(codes_ref[...] > 0.0, total, 0.0)
    sum_ref[...] = jnp.sum(pre_grad, axis=1, keepdims=True)
    code_into(coded_ref, slice(None), pre_grad)


def grad_enc_kernel(count, feats, *refs):
    far, grads, refs = refs[0], refs[1 : 1 + count], refs[1 + count :]
    outs, (inputs_ref, full, grad, arrive) = refs[:count], refs[count:]
    held = Fetched([far], [inputs_ref], arrive)
    for j in range(count):
        full[j * feats : (j + 1) * feats, :] = decoded(grads[j], slice(None))
    upper, lower = split(full[...])
    inputs_ref = held[0]
    dot = functools.partial(
        lax.dot_general,
        dimension_numbers=(((1,), (1,)), ((), ())),
        preferred_element_type=jnp.float32,
    )
    for rows in blocks_of(inputs_ref.shape[0], 256):
        right = inputs_ref[rows, :]
        grad[:, rows] = dot(upper, right) + dot(lower, right)
    for j in range(count):
        code_into(outs[j], slice(None), grad[j * feats : (j + 1) * feats, :])


def local(
    inputs,
    targets,
    enc_weight,
    enc_bias,
    dec_weight,
    dec_bias,
    enc_moments,
    enc_bias_moments,
    dec_moments,
    dec_bias_moments,
    block_lists,
    block_counts,
    slot_block,
):
    inputs_local = inputs[0]
    targets_local = targets[0]
    enc_local = enc_weight[0]
    encb_local = enc_bias[0]
    dec_local = dec_weight[0]
    decb_local = dec_bias[0]
    reach = dec_local.shape[0]
    width, row_count = inputs_local.shape
    feats = enc_local.shape[0]
    count = lax.axis_size("feat")
    block = count * feats
    depth = reach * block
    tile_count = block_counts.shape[1]
    tile_rows = row_count // tile_count
    live = jnp.arange(block_lists.shape[2])[None, :] < block_counts[0][:, None]
    hits = (block_lists[0] == slot_block[0]) & live
    tile_active = jnp.any(hits, axis=1).astype(jnp.float32)
    row_mask = jnp.repeat(tile_active, tile_rows, axis=0)[None, :]

    enc_cols = jnp.concatenate(
        [rotated(slab_of(enc_local, j, width), j) for j in range(count)], axis=0
    )
    me = lax.axis_index("feat").astype(jnp.int32).reshape(1)
    half_way = max(1, reach // 2)
    starts = [(0, half_way)] + [(k, k + 1) for k in range(half_way, reach)]
    dec_cols = []
    for first, last in starts[1:]:
        sent = packed(me, dec_local, first, last)
        dec_cols += [rotated(sent[j], j, first) for j in range(count)]
    partial = jnp.dot(
        enc_cols,
        inputs_local.astype(jnp.float32),
        precision=highest,
        preferred_element_type=jnp.float32,
    ).reshape(count, feats, row_count)
    partials = [rotated(partial[j], -j) for j in range(count)]
    codes, coded_codes = call(
        functools.partial(codes_kernel, count),
        [shape(feats, row_count), coded_shape(feats, row_count)],
        [*partials, encb_local[:, None], row_mask],
        after=[a for i, a in enumerate(dec_cols) if i % count],
    )
    own = [rotated(coded_codes, j) for j in range(count)]
    gathered = call(gather_kernel, [coded_shape(block, row_count)], own)[0]
    moved = [shifted(gathered, "layer", k) for k in range(1, reach)]
    sent = packed(me, dec_local, *starts[0], after=[coded_codes])
    dec_cols = [rotated(sent[j], j) for j in range(count)] + dec_cols
    half = jnp.bfloat16
    weights = call(
        functools.partial(weights_kernel, count, feats, starts),
        [shape(depth, width, half)] * 2,
        [],
        scratch=[buffer_like(a) for a in dec_cols]
        + [pltpu.VMEM((depth, width), jnp.float32), pltpu.SemaphoreType.DMA((len(dec_cols),))],
        far=dec_cols,
    )
    backs = ((0, reach - 1), (reach - 1, reach)) if reach > 1 else ((0, reach),)
    far = [*own, *moved, *weights, decb_local[:, None], targets_local]
    far_out = [shape(block, row_count)] + [coded_shape(block, row_count)] * (reach - 1)
    for first, last in backs:
        far_out += [coded_shape((last - first) * feats, width)] * count
    outs = call(
        functools.partial(main_kernel, count, reach, feats, backs),
        [shape(width, 1)],
        [],
        flops=18 * depth * width * row_count,
        scratch=[buffer_like(a) for a in [*far, *far_out]]
        + [pltpu.VMEM((depth, row_count), jnp.float32), pltpu.VMEM((depth, width), jnp.float32)]
        + [pltpu.VMEM((width, row_count), half)] * 2
        + [pltpu.VMEM((depth, row_count), half)] * 2
        + [pltpu.SemaphoreType.DMA((len(far),)), pltpu.SemaphoreType.DMA((len(far_out),))],
        far=far,
        far_out=far_out,
    )
    part, parts, grad_parts, grad_dec_bias = outs[0], outs[1:reach], outs[reach:-1], outs[-1]
    returned = [shifted(parts[k - 1], "layer", -k) for k in range(1, reach)]
    grad_dec_cols = [
        [rotated(grad_parts[i * count + j], -j, first if i else 0) for j in range(count)]
        for i, (first, last) in enumerate(backs)
    ]
    sums = call(
        functools.partial(code_sum_kernel, count, feats, reach - 1),
        [shape(feats, row_count)] + [coded_shape(feats, row_count)] * (count - 1),
        [part, *returned],
    )
    arrived = [rotated(sums[j], -j) for j in range(count)]
    coded_grad, grad_enc_bias = call(
        functools.partial(pre_grad_kernel, count),
        [coded_shape(feats, row_count), shape(feats, 1)],
        [*arrived, codes],
        after=grad_dec_cols[0][1:],
    )
    pre_grads = [rotated(coded_grad, j) for j in range(count)]
    grad_enc_cols = call(
        functools.partial(grad_enc_kernel, count, feats),
        [coded_shape(feats, width)] * count,
        pre_grads,
        flops=4 * block * width * row_count,
        scratch=[
            buffer_like(inputs_local),
            pltpu.VMEM((block, row_count), jnp.float32),
            pltpu.VMEM((block, width), jnp.float32),
            pltpu.SemaphoreType.DMA((1,)),
        ],
        far=[inputs_local],
        alone=False,
    )
    dec_done = ()
    for (first, last), grads in zip(backs, grad_dec_cols):
        dec_done = adam_call(
            me, first, last, grads, dec_local, dec_moments[:, 0], dec_done, [grad_enc_cols[0]]
        )
    dec_new, dec_mom = dec_done
    enc_arrived = [rotated(grad_enc_cols[j], -j) for j in range(count)]
    enc_new, enc_mom = adam_call(me, 0, 1, enc_arrived, enc_local[None], enc_moments)
    encb_new, encb_mom = adam_update(encb_local, enc_bias_moments[:, 0], grad_enc_bias[:, 0])
    decb_new, decb_mom = adam_update(decb_local, dec_bias_moments[:, 0], grad_dec_bias[:, 0])
    return (
        enc_new,
        encb_new[None],
        dec_new[None],
        decb_new[None],
        enc_mom,
        encb_mom[:, None],
        dec_mom[:, None],
        decb_mom[:, None],
    )


def solution(mesh):
    cols = P(("group", "layer"), "feat", None)
    vec = P(("group", "layer"), "feat")
    dec = P(("group", "layer"), None, "feat", None)
    cols_mom = P(None, ("group", "layer"), "feat", None)
    vec_mom = P(None, ("group", "layer"), "feat")
    dec_mom = P(None, ("group", "layer"), None, "feat", None)
    return jax.shard_map(
        local,
        mesh=mesh,
        in_specs=(
            cols,
            cols,
            cols,
            vec,
            dec,
            vec,
            cols_mom,
            vec_mom,
            dec_mom,
            vec_mom,
            P(("group", "layer"), None, None),
            P(("group", "layer"), None),
            P(("group", "layer")),
        ),
        out_specs=(cols, vec, dec, vec, cols_mom, vec_mom, dec_mom, vec_mom),
        check_vma=False,
    )
```

```python
import functools

import jax
import jax.numpy as jnp
from jax import lax
from jax.experimental import pallas as pl
from jax.experimental.pallas import tpu as pltpu
from jax.sharding import PartitionSpec as P

beta_one = 0.9
beta_two = 0.999
learn_rate = 0.001
adam_eps = 1e-08
step_count = 100.0
lanes = 128
log_two = 0.6931471805599453
levels = 32767.0
vmem_bytes = 60 * 1024 * 1024
held_types = (jnp.float32, jnp.bfloat16, jnp.int16)


def shifted(value, axis, steps):
    count = lax.axis_size(axis)
    initial, last = (max(0, -steps), min(count, count - steps))
    return lax.ppermute(value, axis, [(source, source + steps) for source in range(initial, last)])


def rotated(value, steps, first_layer=0):
    count = lax.axis_size("feat")
    steps = steps % count
    if steps == 0:
        return value
    pairs = [
        (layer * count + s, layer * count + (s + steps) % count)
        for layer in range(first_layer, lax.axis_size("layer"))
        for s in range(count)
    ]
    return lax.ppermute(value, ("layer", "feat"), pairs)


def adam_update(weight, moments, grad):
    first = beta_one * moments[0] + (1.0 - beta_one) * grad
    second = beta_two * moments[1] + (1.0 - beta_two) * grad * grad
    scaled_first = first / (1.0 - beta_one**step_count)
    scaled_second = second / (1.0 - beta_two**step_count)
    updated = weight - learn_rate * scaled_first / (jnp.sqrt(scaled_second) + adam_eps)
    return (updated, jnp.stack([first, second]))


def slab_of(value, steps, width):
    count = lax.axis_size("feat")
    place = lax.rem(lax.axis_index("feat") + steps, count) * width
    return lax.dynamic_slice_in_dim(value, place, width, axis=value.ndim - 1)


exponent_bits = 12
exponent_offset = 1024


def lane_index(rows):
    return lax.broadcasted_iota(jnp.int32, (rows, lanes), 1)


def code_into(out_ref, rows, value):
    count, width = value.shape
    top = jnp.max(jnp.abs(value), axis=1, keepdims=True)
    exponent = jnp.ceil(jnp.log(jnp.maximum(top, 1e-30)) * (8.0 / log_two))
    scale = levels * jnp.exp(exponent * (-log_two / 8.0))
    whole = jnp.clip(jnp.round(value * scale), -levels, levels).astype(jnp.int32)
    lane = lane_index(count)
    shown = jnp.broadcast_to(exponent.astype(jnp.int32) + exponent_offset, (count, lanes))
    bits = lax.shift_right_logical(shown, jnp.minimum(lane, exponent_bits)) & 1
    first = whole[:, 0:lanes]
    first = jnp.where(lane < exponent_bits, (first & -2) | bits, first)
    out_ref[rows, 0:lanes] = first.astype(jnp.int16)
    if width > lanes:
        out_ref[rows, lanes:width] = whole[:, lanes:width].astype(jnp.int16)


def decoded(ref, rows):
    whole = ref[rows, :].astype(jnp.int32)
    count = whole.shape[0]
    lane = lane_index(count)
    bits = lax.shift_left(whole[:, 0:lanes] & 1, jnp.minimum(lane, exponent_bits))
    bits = jnp.where(lane < exponent_bits, bits, 0).astype(jnp.float32)
    exponent = jnp.sum(bits, axis=1, keepdims=True) - exponent_offset
    step = jnp.exp(jnp.maximum(exponent, -880.0) * (log_two / 8.0)) * (1.0 / levels)
    return whole.astype(jnp.float32) * step


def split(value):
    upper = value.astype(jnp.bfloat16)
    return upper, (value - upper.astype(jnp.float32)).astype(jnp.bfloat16)


def product(left, right, dims):
    dot = functools.partial(
        lax.dot_general, dimension_numbers=(dims, ((), ())), preferred_element_type=jnp.float32
    )
    return dot(left[0], right[0]) + (dot(left[0], right[1]) + dot(left[1], right[0]))


def blocks_of(size, block):
    block = min(size, block)
    return [slice(start, start + block) for start in range(0, size, block)]


def held_bytes(array):
    size = array.dtype.itemsize
    if len(array.shape) == 1:
        return 4096
    rows, columns = array.shape[-2:]
    tile = 32 // size
    rows, columns = -(-rows // tile) * tile, -(-columns // lanes) * lanes
    for extent in array.shape[:-2]:
        rows = rows * extent
    return rows * columns * size


def call(kernel, out_shape, args, flops=0, scratch=(), after=(), far=(), far_out=(), alone=True):
    size = sum(a.size * a.dtype.itemsize for a in [*far, *args])
    size += sum(o.size * o.dtype.itemsize for o in [*far_out, *out_shape])
    distant, taken, skipped = len(far), len(args), len(after)
    need = sum(held_bytes(a) for a in [*args, *out_shape]) + 4 * 1024 * 1024
    need += sum(held_bytes(a) for a in scratch if a.dtype in held_types)

    def body(*refs):
        kernel(*refs[: distant + taken], *refs[distant + taken + skipped :])

    spaces = [pltpu.HBM] * distant
    spaces += [pltpu.SMEM if a.shape == (1,) else pltpu.VMEM for a in args]
    spaces += [pl.ANY] * skipped
    out_spaces = [pltpu.HBM] * len(far_out) + [pltpu.VMEM] * len(out_shape)
    return pl.pallas_call(
        body,
        out_shape=(*far_out, *out_shape),
        in_specs=[pl.BlockSpec(memory_space=space) for space in spaces],
        out_specs=tuple(pl.BlockSpec(memory_space=space) for space in out_spaces),
        scratch_shapes=list(scratch),
        cost_estimate=pl.CostEstimate(flops=flops, bytes_accessed=size, transcendentals=0),
        compiler_params=pltpu.CompilerParams(vmem_limit_bytes=max(need, vmem_bytes if far and alone else 0)),
    )(*far, *args, *after)


def buffer_like(array):
    return pltpu.VMEM(array.shape, array.dtype)


class Fetched:
    def __init__(self, sources, buffers, semaphores):
        self.copies = [
            pltpu.make_async_copy(source, held, semaphores.at[i])
            for i, (source, held) in enumerate(zip(sources, buffers, strict=True))
        ]
        self.buffers = buffers
        for copy in self.copies:
            copy.start()

    def __getitem__(self, i):
        self.copies[i].wait()
        return self.buffers[i]


def shape(rows, columns, dtype=jnp.float32):
    return jax.ShapeDtypeStruct((rows, columns), dtype)


def coded_shape(rows, columns):
    return jax.ShapeDtypeStruct((rows, columns), jnp.int16)


def pack_kernel(count, first, last, me_ref, in_ref, *outs):
    reach, feats, total = in_ref.shape
    width = total // count
    for j in range(count):
        place = pl.multiple_of(lax.rem(me_ref[0] + j, count) * width, lanes)
        for k in range(first, last):
            rows = slice((k - first) * feats, (k - first + 1) * feats)
            code_into(outs[j], rows, in_ref[k, :, pl.ds(place, width)])


def packed(me, weights, first, last, after=()):
    count = lax.axis_size("feat")
    reach, feats, total = weights.shape
    out = coded_shape((last - first) * feats, total // count)
    kernel = functools.partial(pack_kernel, count, first, last)
    return call(kernel, [out] * count, [me, weights], after=after)


def adam_kernel(count, me_ref, *refs):
    grads, (weight_ref, moments_ref), (new_ref, new_moments_ref) = refs[:count], refs[count : count + 2], refs[-2:]
    width = weight_ref.shape[2] // count
    for j in range(count):
        place = pl.multiple_of(lax.rem(me_ref[0] + j, count) * width, lanes)
        cols = pl.ds(place, width)
        grad = decoded(grads[j], slice(None))
        first = beta_one * moments_ref[0, 0, :, cols] + (1.0 - beta_one) * grad
        second = beta_two * moments_ref[1, 0, :, cols] + (1.0 - beta_two) * grad * grad
        new_moments_ref[0, 0, :, cols] = first
        new_moments_ref[1, 0, :, cols] = second
        scaled_first = first * (learn_rate / (1.0 - beta_one**step_count))
        scaled_second = second * (1.0 / (1.0 - beta_two**step_count))
        new_ref[0, :, cols] = weight_ref[0, :, cols] - scaled_first / (
            jnp.sqrt(scaled_second) + adam_eps
        )


def adam_call(me, start, stop, grads, weight, moments, filled=(), after=()):
    count = lax.axis_size("feat")
    feats, total = weight.shape[1:]
    grad_spec = pl.BlockSpec((feats, total // count), lambda k: (k, 0))
    weight_spec = pl.BlockSpec((1, feats, total), lambda k: (start + k, 0, 0))
    moments_spec = pl.BlockSpec((2, 1, feats, total), lambda k: (0, start + k, 0, 0))
    place = 1 + count + 2
    return pl.pallas_call(
        functools.partial(adam_kernel, count),
        grid=(stop - start,),
        out_shape=(
            jax.ShapeDtypeStruct(weight.shape, weight.dtype),
            jax.ShapeDtypeStruct(moments.shape, moments.dtype),
        ),
        in_specs=[pl.BlockSpec(memory_space=pltpu.SMEM)]
        + [grad_spec] * count
        + [weight_spec, moments_spec]
        + [pl.BlockSpec(memory_space=pl.ANY)] * (len(filled) + len(after)),
        out_specs=(weight_spec, moments_spec),
        input_output_aliases={place + i: i for i in range(len(filled))},
        cost_estimate=pl.CostEstimate(
            flops=20 * (stop - start) * feats * total,
            bytes_accessed=26 * (stop - start) * feats * total,
            transcendentals=(stop - start) * feats * total,
        ),
        compiler_params=pltpu.CompilerParams(
            vmem_limit_bytes=24 * 1024 * 1024
        ),
    )(me, *grads, weight, moments, *filled, *after)


def gather_kernel(*refs):
    *parts, out_ref = refs
    feats = parts[0].shape[0]
    for j, part in enumerate(parts):
        out_ref[j * feats : (j + 1) * feats, :] = part[...]


def exact_add(total, lost, term):
    added = total + term
    seen = added - total
    return added, lost + ((total - (added - seen)) + (term - seen))


def partial_kernel(count, *refs):
    encs, inputs_ref, outs, full = refs[:count], refs[count], refs[count + 1 : -1], refs[-1]
    feats = encs[0].shape[0]
    for j in range(count):
        full[j * feats : (j + 1) * feats, :] = encs[j][...]
    upper = full[...].astype(jnp.bfloat16)
    rest = full[...] - upper.astype(jnp.float32)
    middle = rest.astype(jnp.bfloat16)
    lower = (rest - middle.astype(jnp.float32)).astype(jnp.bfloat16)
    total, lost = None, 0.0
    for cols in blocks_of(full.shape[1], 256):
        right = inputs_ref[cols, :]
        term, fine, finest = (
            jnp.dot(left[:, cols], right, preferred_element_type=jnp.float32)
            for left in (upper, middle, lower)
        )
        lost = lost + (fine + finest)
        if total is None:
            total = term
        else:
            total, lost = exact_add(total, lost, term)
    total = total + lost
    for j in range(count):
        outs[j][...] = total[j * feats : (j + 1) * feats, :]


def codes_kernel(count, *refs):
    parts, bias_ref, mask_ref, codes_ref, coded_ref = refs[:count], *refs[count:]
    pre, lost = parts[0][...], 0.0
    for part in parts[1:]:
        pre, lost = exact_add(pre, lost, part[...])
    pre, lost = exact_add(pre, lost, jnp.broadcast_to(bias_ref[...], pre.shape))
    pre = pre + lost
    codes = jnp.maximum(pre, 0.0) * mask_ref[...]
    codes_ref[...] = codes
    code_into(coded_ref, slice(None), codes)


def weights_kernel(count, feats, starts, *refs):
    parts = len(starts)
    fars, refs = refs[: parts * count], refs[parts * count :]
    (up_ref, low_ref), (*buffers, full, arrive) = refs[:2], refs[2:]
    held = Fetched(fars, buffers, arrive)
    for part, (start, stop) in enumerate(starts):
        for j in range(count):
            weights = held[part * count + j]
            for k in range(start, stop):
                row = ((k - starts[0][0]) * count + j) * feats
                rows = slice((k - start) * feats, (k - start + 1) * feats)
                full[row : row + feats, :] = decoded(weights, rows)
    for rows in blocks_of(full.shape[0], 32):
        up_ref[rows, :], low_ref[rows, :] = split(full[rows, :])


def main_kernel(count, reach, feats, starts, pieces, lates, *refs):
    fetched = count * len(lates)
    sources = count + reach - 1 + 2 * len(pieces) + fetched + 2
    results = reach + len(starts) * count
    fars, far_outs, sum_ref = refs[:sources], refs[sources : sources + results], refs[sources + results]
    refs = refs[sources + results + 1 :]
    plain = count + reach - 1
    buffers, refs = refs[: plain + fetched + 2], refs[plain + fetched + 2 :]
    outs, refs = refs[:results], refs[results:]
    full, grad, w_up, w_low, res_up, res_low, src_up, src_low, arrive, leave = refs
    block = count * feats
    places = [pl.ds(start * block, (stop - start) * block) for start, stop in pieces]
    rooms = [ref.at[place] for place in places for ref in (w_up, w_low)]
    held = Fetched(fars, [*buffers[:plain], *rooms, *buffers[plain:]], arrive)
    sends = [
        pltpu.make_async_copy(source, out, leave.at[i])
        for i, (source, out) in enumerate(zip(outs, far_outs, strict=True))
    ]
    for j in range(count):
        full[j * feats : (j + 1) * feats, :] = decoded(held[j], slice(None))
    for k in range(1, reach):
        moved = held[count + k - 1]
        for rows in blocks_of(block, 32):
            full[k * block + rows.start : k * block + rows.stop, :] = decoded(moved, rows)
    for rows in blocks_of(reach * block, 32):
        src_up[rows, :], src_low[rows, :] = split(full[rows, :])
    for i in range(2 * len(pieces)):
        held[plain + i]
    for part, (start, stop) in enumerate(lates):
        for j in range(count):
            weights = held[plain + 2 * len(pieces) + part * count + j]
            for k in range(start, stop):
                row = (k * count + j) * feats
                rows = slice((k - start) * feats, (k - start + 1) * feats)
                grad[row : row + feats, :] = decoded(weights, rows)
        for rows in blocks_of((stop - start) * block, 32):
            rows = slice(start * block + rows.start, start * block + rows.stop)
            w_up[rows, :], w_low[rows, :] = split(grad[rows, :])
    bias_ref, targets_ref = held[sources - 2], held[sources - 1]
    width, row_count = targets_ref.shape
    for cols in blocks_of(width, 256):
        recon = product(
            (w_up[:, cols], w_low[:, cols]), (src_up[...], src_low[...]), ((0,), (0,))
        )
        resid = recon + bias_ref[cols, :] - targets_ref[cols, :].astype(jnp.float32)
        sum_ref[cols, :] = jnp.sum(resid, axis=1, keepdims=True)
        res_up[cols, :], res_low[cols, :] = split(resid)
    for cols in blocks_of(row_count, 256):
        full[:, cols] = product(
            (w_up[...], w_low[...]), (res_up[:, cols], res_low[:, cols]), ((1,), (0,))
        )
    outs[0][...] = full[0:block, :]
    sends[0].start()
    for k in range(1, reach):
        for rows in blocks_of(block, 32):
            source = slice(k * block + rows.start, k * block + rows.stop)
            code_into(outs[k], rows, full[source, :])
        sends[k].start()
    for part, (start, stop) in enumerate(starts):
        held_rows = slice(start * block, stop * block)
        for rows in blocks_of(width, 256):
            grad[held_rows, rows] = product(
                (src_up[held_rows, :], src_low[held_rows, :]),
                (res_up[rows, :], res_low[rows, :]),
                ((1,), (1,)),
            )
        for j in range(count):
            place = reach + part * count + j
            for k in range(start, stop):
                row = (k * count + j) * feats
                rows = slice((k - start) * feats, (k - start + 1) * feats)
                code_into(outs[place], rows, grad[row : row + feats, :])
            sends[place].start()
    for send in sends:
        send.wait()


def code_sum_kernel(count, feats, moved_count, *refs):
    codes_ref, kept_ref = refs[0], refs[-1]
    own, moved, outs = refs[1], refs[2 : 2 + moved_count], refs[2 + moved_count : -1]
    kept_ref[...] = codes_ref[...]
    for j in range(count):
        rows = slice(j * feats, (j + 1) * feats)
        total = own[rows, :]
        for ref in moved:
            total = total + decoded(ref, rows)
        if j == 0:
            outs[0][...] = total
        else:
            code_into(outs[j], slice(None), total)


def pre_grad_kernel(count, *refs):
    own, arrived, codes_ref, coded_ref, sum_ref = refs[0], refs[1:count], *refs[count:]
    total = own[...]
    for ref in arrived:
        total = total + decoded(ref, slice(None))
    pre_grad = jnp.where(codes_ref[...] > 0.0, total, 0.0)
    sum_ref[...] = jnp.sum(pre_grad, axis=1, keepdims=True)
    code_into(coded_ref, slice(None), pre_grad)


def grad_enc_kernel(count, feats, *refs):
    far, grads, refs = refs[0], refs[1 : 1 + count], refs[1 + count :]
    outs, (inputs_ref, full, grad, arrive) = refs[:count], refs[count:]
    held = Fetched([far], [inputs_ref], arrive)
    for j in range(count):
        full[j * feats : (j + 1) * feats, :] = decoded(grads[j], slice(None))
    upper, lower = split(full[...])
    inputs_ref = held[0]
    dot = functools.partial(
        lax.dot_general,
        dimension_numbers=(((1,), (1,)), ((), ())),
        preferred_element_type=jnp.float32,
    )
    for rows in blocks_of(inputs_ref.shape[0], 256):
        right = inputs_ref[rows, :]
        grad[:, rows] = dot(upper, right) + dot(lower, right)
    for j in range(count):
        code_into(outs[j], slice(None), grad[j * feats : (j + 1) * feats, :])


def local(
    inputs,
    targets,
    enc_weight,
    enc_bias,
    dec_weight,
    dec_bias,
    enc_moments,
    enc_bias_moments,
    dec_moments,
    dec_bias_moments,
    block_lists,
    block_counts,
    slot_block,
):
    inputs_local = inputs[0]
    targets_local = targets[0]
    enc_local = enc_weight[0]
    encb_local = enc_bias[0]
    dec_local = dec_weight[0]
    decb_local = dec_bias[0]
    reach = dec_local.shape[0]
    width, row_count = inputs_local.shape
    feats = enc_local.shape[0]
    count = lax.axis_size("feat")
    block = count * feats
    depth = reach * block
    tile_count = block_counts.shape[1]
    tile_rows = row_count // tile_count
    live = jnp.arange(block_lists.shape[2])[None, :] < block_counts[0][:, None]
    hits = (block_lists[0] == slot_block[0]) & live
    tile_active = jnp.any(hits, axis=1).astype(jnp.float32)
    row_mask = jnp.repeat(tile_active, tile_rows, axis=0)[None, :]

    enc_cols = [rotated(slab_of(enc_local, j, width), j) for j in range(count)]
    me = lax.axis_index("feat").astype(jnp.int32).reshape(1)
    half_way = max(1, reach // 2)
    sent = packed(me, dec_local, 0, half_way)
    early = [rotated(sent[j], j) for j in range(count)]
    partial = call(
        functools.partial(partial_kernel, count),
        [shape(feats, row_count)] * count,
        [*enc_cols, inputs_local],
        flops=6 * block * width * row_count,
        scratch=[pltpu.VMEM((block, width), jnp.float32)],
    )
    partials = [rotated(partial[j], -j) for j in range(count)]
    codes, coded_codes = call(
        functools.partial(codes_kernel, count),
        [shape(feats, row_count), coded_shape(feats, row_count)],
        [*partials, encb_local[:, None], row_mask],
        after=early[1:],
    )
    own = [rotated(coded_codes, j) for j in range(count)]
    half = jnp.bfloat16

    def weights_of(starts, columns):
        rows = (starts[-1][1] - starts[0][0]) * block
        return call(
            functools.partial(weights_kernel, count, feats, starts),
            [shape(rows, width, half)] * 2,
            [],
            scratch=[buffer_like(a) for a in columns]
            + [pltpu.VMEM((rows, width), jnp.float32), pltpu.SemaphoreType.DMA((len(columns),))],
            far=columns,
        )

    pieces = [(0, half_way)]
    weights = [*weights_of(pieces, early)]
    gathered = call(gather_kernel, [coded_shape(block, row_count)], own, after=weights[:1])[0]
    moved = [shifted(gathered, "layer", k) for k in range(1, reach)]
    late, lates = [], [(half_way, reach)] if half_way < reach else []
    for first, last in lates:
        sent = packed(me, dec_local, first, last, after=[coded_codes])
        late += [rotated(sent[j], j, first) for j in range(count)]
    backs = (*pieces, *lates)
    far = [*own, *moved, *weights, *late, decb_local[:, None], targets_local]
    far_out = [shape(block, row_count)] + [coded_shape(block, row_count)] * (reach - 1)
    for first, last in backs:
        far_out += [coded_shape((last - first) * feats, width)] * count
    outs = call(
        functools.partial(main_kernel, count, reach, feats, backs, pieces, lates),
        [shape(width, 1)],
        [],
        flops=18 * depth * width * row_count,
        scratch=[buffer_like(a) for a in [*own, *moved, *late, *far[-2:], *far_out]]
        + [pltpu.VMEM((depth, row_count), jnp.float32), pltpu.VMEM((depth, width), jnp.float32)]
        + [pltpu.VMEM((depth, width), half)] * 2
        + [pltpu.VMEM((width, row_count), half)] * 2
        + [pltpu.VMEM((depth, row_count), half)] * 2
        + [pltpu.SemaphoreType.DMA((len(far),)), pltpu.SemaphoreType.DMA((len(far_out),))],
        far=far,
        far_out=far_out,
    )
    part, parts, grad_parts, grad_dec_bias = outs[0], outs[1:reach], outs[reach:-1], outs[-1]
    returned = [shifted(parts[k - 1], "layer", -k) for k in range(1, reach)]
    grad_dec_cols = [
        [rotated(grad_parts[i * count + j], -j, first if i else 0) for j in range(count)]
        for i, (first, last) in enumerate(backs)
    ]
    sums = call(
        functools.partial(code_sum_kernel, count, feats, reach - 1),
        [shape(feats, row_count)]
        + [coded_shape(feats, row_count)] * (count - 1)
        + [shape(feats, row_count)],
        [codes, part, *returned],
    )
    arrived = [rotated(sums[j], -j) for j in range(count)]
    coded_grad, grad_enc_bias = call(
        functools.partial(pre_grad_kernel, count),
        [coded_shape(feats, row_count), shape(feats, 1)],
        [*arrived, sums[-1]],
        after=grad_dec_cols[0][1:],
    )
    dec_done = adam_call(
        me, *backs[0], grad_dec_cols[0], dec_local, dec_moments[:, 0], after=[coded_grad]
    )
    pre_grads = [rotated(coded_grad, j) for j in range(count)]
    grad_enc_cols = call(
        functools.partial(grad_enc_kernel, count, feats),
        [coded_shape(feats, width)] * count,
        pre_grads,
        flops=4 * block * width * row_count,
        scratch=[
            buffer_like(inputs_local),
            pltpu.VMEM((block, row_count), jnp.float32),
            pltpu.VMEM((block, width), jnp.float32),
            pltpu.SemaphoreType.DMA((1,)),
        ],
        after=dec_done[:1],
        far=[inputs_local],
        alone=False,
    )
    for (first, last), grads in zip(backs[1:], grad_dec_cols[1:]):
        dec_done = adam_call(
            me, first, last, grads, dec_local, dec_moments[:, 0], dec_done, [grad_enc_cols[0]]
        )
    dec_new, dec_mom = dec_done
    enc_arrived = [rotated(grad_enc_cols[j], -j) for j in range(count)]
    enc_new, enc_mom = adam_call(me, 0, 1, enc_arrived, enc_local[None], enc_moments)
    encb_new, encb_mom = adam_update(encb_local, enc_bias_moments[:, 0], grad_enc_bias[:, 0])
    decb_new, decb_mom = adam_update(decb_local, dec_bias_moments[:, 0], grad_dec_bias[:, 0])
    return (
        enc_new,
        encb_new[None],
        dec_new[None],
        decb_new[None],
        enc_mom,
        encb_mom[:, None],
        dec_mom[:, None],
        decb_mom[:, None],
    )


def solution(mesh):
    cols = P(("group", "layer"), "feat", None)
    vec = P(("group", "layer"), "feat")
    dec = P(("group", "layer"), None, "feat", None)
    cols_mom = P(None, ("group", "layer"), "feat", None)
    vec_mom = P(None, ("group", "layer"), "feat")
    dec_mom = P(None, ("group", "layer"), None, "feat", None)
    return jax.shard_map(
        local,
        mesh=mesh,
        in_specs=(
            cols,
            cols,
            cols,
            vec,
            dec,
            vec,
            cols_mom,
            vec_mom,
            dec_mom,
            vec_mom,
            P(("group", "layer"), None, None),
            P(("group", "layer"), None),
            P(("group", "layer")),
        ),
        out_specs=(cols, vec, dec, vec, cols_mom, vec_mom, dec_mom, vec_mom),
        check_vma=False,
    )
```

```python
import functools

import jax
import jax.numpy as jnp
from jax import lax
from jax.experimental import pallas as pl
from jax.experimental.pallas import tpu as pltpu
from jax.sharding import PartitionSpec as P

beta_one = 0.9
beta_two = 0.999
learn_rate = 0.001
adam_eps = 1e-08
step_count = 100.0
lanes = 128
log_two = 0.6931471805599453
levels = 32767.0
vmem_bytes = 60 * 1024 * 1024
held_types = (jnp.float32, jnp.bfloat16, jnp.int16)


def shifted(value, axis, steps):
    count = lax.axis_size(axis)
    initial, last = (max(0, -steps), min(count, count - steps))
    return lax.ppermute(value, axis, [(source, source + steps) for source in range(initial, last)])


def rotated(value, steps, first_layer=0):
    count = lax.axis_size("feat")
    steps = steps % count
    if steps == 0:
        return value
    pairs = [
        (layer * count + s, layer * count + (s + steps) % count)
        for layer in range(first_layer, lax.axis_size("layer"))
        for s in range(count)
    ]
    return lax.ppermute(value, ("layer", "feat"), pairs)


def adam_update(weight, moments, grad):
    first = beta_one * moments[0] + (1.0 - beta_one) * grad
    second = beta_two * moments[1] + (1.0 - beta_two) * grad * grad
    scaled_first = first / (1.0 - beta_one**step_count)
    scaled_second = second / (1.0 - beta_two**step_count)
    updated = weight - learn_rate * scaled_first / (jnp.sqrt(scaled_second) + adam_eps)
    return (updated, jnp.stack([first, second]))


def slab_of(value, steps, width):
    count = lax.axis_size("feat")
    place = lax.rem(lax.axis_index("feat") + steps, count) * width
    return lax.dynamic_slice_in_dim(value, place, width, axis=value.ndim - 1)


exponent_bits = 12
exponent_offset = 1024


def lane_index(rows):
    return lax.broadcasted_iota(jnp.int32, (rows, lanes), 1)


def code_into(out_ref, rows, value):
    count, width = value.shape
    top = jnp.max(jnp.abs(value), axis=1, keepdims=True)
    exponent = jnp.ceil(jnp.log(jnp.maximum(top, 1e-30)) * (8.0 / log_two))
    scale = levels * jnp.exp(exponent * (-log_two / 8.0))
    whole = jnp.clip(jnp.round(value * scale), -levels, levels).astype(jnp.int32)
    lane = lane_index(count)
    shown = jnp.broadcast_to(exponent.astype(jnp.int32) + exponent_offset, (count, lanes))
    bits = lax.shift_right_logical(shown, jnp.minimum(lane, exponent_bits)) & 1
    first = whole[:, 0:lanes]
    first = jnp.where(lane < exponent_bits, (first & -2) | bits, first)
    out_ref[rows, 0:lanes] = first.astype(jnp.int16)
    if width > lanes:
        out_ref[rows, lanes:width] = whole[:, lanes:width].astype(jnp.int16)


def decoded(ref, rows):
    whole = ref[rows, :].astype(jnp.int32)
    count = whole.shape[0]
    lane = lane_index(count)
    bits = lax.shift_left(whole[:, 0:lanes] & 1, jnp.minimum(lane, exponent_bits))
    bits = jnp.where(lane < exponent_bits, bits, 0).astype(jnp.float32)
    exponent = jnp.sum(bits, axis=1, keepdims=True) - exponent_offset
    step = jnp.exp(jnp.maximum(exponent, -880.0) * (log_two / 8.0)) * (1.0 / levels)
    return whole.astype(jnp.float32) * step


def split(value):
    upper = value.astype(jnp.bfloat16)
    return upper, (value - upper.astype(jnp.float32)).astype(jnp.bfloat16)


def product(left, right, dims):
    dot = functools.partial(
        lax.dot_general, dimension_numbers=(dims, ((), ())), preferred_element_type=jnp.float32
    )
    return dot(left[0], right[0]) + (dot(left[0], right[1]) + dot(left[1], right[0]))


def blocks_of(size, block):
    block = min(size, block)
    return [slice(start, start + block) for start in range(0, size, block)]


def held_bytes(array):
    size = array.dtype.itemsize
    if len(array.shape) == 1:
        return 4096
    rows, columns = array.shape[-2:]
    tile = 32 // size
    rows, columns = -(-rows // tile) * tile, -(-columns // lanes) * lanes
    for extent in array.shape[:-2]:
        rows = rows * extent
    return rows * columns * size


def call(kernel, out_shape, args, flops=0, scratch=(), after=(), far=(), far_out=(), alone=True):
    size = sum(a.size * a.dtype.itemsize for a in [*far, *args])
    size += sum(o.size * o.dtype.itemsize for o in [*far_out, *out_shape])
    distant, taken, skipped = len(far), len(args), len(after)
    need = sum(held_bytes(a) for a in [*args, *out_shape]) + 4 * 1024 * 1024
    need += sum(held_bytes(a) for a in scratch if a.dtype in held_types)

    def body(*refs):
        kernel(*refs[: distant + taken], *refs[distant + taken + skipped :])

    spaces = [pltpu.HBM] * distant
    spaces += [pltpu.SMEM if a.shape == (1,) else pltpu.VMEM for a in args]
    spaces += [pl.ANY] * skipped
    out_spaces = [pltpu.HBM] * len(far_out) + [pltpu.VMEM] * len(out_shape)
    return pl.pallas_call(
        body,
        out_shape=(*far_out, *out_shape),
        in_specs=[pl.BlockSpec(memory_space=space) for space in spaces],
        out_specs=tuple(pl.BlockSpec(memory_space=space) for space in out_spaces),
        scratch_shapes=list(scratch),
        cost_estimate=pl.CostEstimate(flops=flops, bytes_accessed=size, transcendentals=0),
        compiler_params=pltpu.CompilerParams(vmem_limit_bytes=max(need, vmem_bytes if far and alone else 0)),
    )(*far, *args, *after)


def buffer_like(array):
    return pltpu.VMEM(array.shape, array.dtype)


class Fetched:
    def __init__(self, sources, buffers, semaphores):
        self.copies = [
            pltpu.make_async_copy(source, held, semaphores.at[i])
            for i, (source, held) in enumerate(zip(sources, buffers, strict=True))
        ]
        self.buffers = buffers
        for copy in self.copies:
            copy.start()

    def __getitem__(self, i):
        self.copies[i].wait()
        return self.buffers[i]


def shape(rows, columns, dtype=jnp.float32):
    return jax.ShapeDtypeStruct((rows, columns), dtype)


def coded_shape(rows, columns):
    return jax.ShapeDtypeStruct((rows, columns), jnp.int16)


def pack_kernel(count, first, last, me_ref, in_ref, *outs):
    reach, feats, total = in_ref.shape
    width = total // count
    for j in range(count):
        place = pl.multiple_of(lax.rem(me_ref[0] + j, count) * width, lanes)
        for k in range(first, last):
            rows = slice((k - first) * feats, (k - first + 1) * feats)
            code_into(outs[j], rows, in_ref[k, :, pl.ds(place, width)])


def packed(me, weights, first, last, after=()):
    count = lax.axis_size("feat")
    reach, feats, total = weights.shape
    out = coded_shape((last - first) * feats, total // count)
    kernel = functools.partial(pack_kernel, count, first, last)
    return call(kernel, [out] * count, [me, weights], after=after)


def adam_kernel(count, me_ref, *refs):
    grads, (weight_ref, moments_ref), (new_ref, new_moments_ref) = refs[:count], refs[count : count + 2], refs[-2:]
    width = weight_ref.shape[2] // count
    for j in range(count):
        place = pl.multiple_of(lax.rem(me_ref[0] + j, count) * width, lanes)
        cols = pl.ds(place, width)
        grad = decoded(grads[j], slice(None))
        first = beta_one * moments_ref[0, 0, :, cols] + (1.0 - beta_one) * grad
        second = beta_two * moments_ref[1, 0, :, cols] + (1.0 - beta_two) * grad * grad
        new_moments_ref[0, 0, :, cols] = first
        new_moments_ref[1, 0, :, cols] = second
        scaled_first = first * (learn_rate / (1.0 - beta_one**step_count))
        scaled_second = second * (1.0 / (1.0 - beta_two**step_count))
        new_ref[0, :, cols] = weight_ref[0, :, cols] - scaled_first / (
            jnp.sqrt(scaled_second) + adam_eps
        )


def adam_call(me, start, stop, grads, weight, moments, filled=(), after=()):
    count = lax.axis_size("feat")
    feats, total = weight.shape[1:]
    grad_spec = pl.BlockSpec((feats, total // count), lambda k: (k, 0))
    weight_spec = pl.BlockSpec((1, feats, total), lambda k: (start + k, 0, 0))
    moments_spec = pl.BlockSpec((2, 1, feats, total), lambda k: (0, start + k, 0, 0))
    place = 1 + count + 2
    return pl.pallas_call(
        functools.partial(adam_kernel, count),
        grid=(stop - start,),
        out_shape=(
            jax.ShapeDtypeStruct(weight.shape, weight.dtype),
            jax.ShapeDtypeStruct(moments.shape, moments.dtype),
        ),
        in_specs=[pl.BlockSpec(memory_space=pltpu.SMEM)]
        + [grad_spec] * count
        + [weight_spec, moments_spec]
        + [pl.BlockSpec(memory_space=pl.ANY)] * (len(filled) + len(after)),
        out_specs=(weight_spec, moments_spec),
        input_output_aliases={place + i: i for i in range(len(filled))},
        cost_estimate=pl.CostEstimate(
            flops=20 * (stop - start) * feats * total,
            bytes_accessed=26 * (stop - start) * feats * total,
            transcendentals=(stop - start) * feats * total,
        ),
        compiler_params=pltpu.CompilerParams(
            vmem_limit_bytes=24 * 1024 * 1024
        ),
    )(me, *grads, weight, moments, *filled, *after)


def gather_kernel(*refs):
    *parts, out_ref = refs
    feats = parts[0].shape[0]
    for j, part in enumerate(parts):
        out_ref[j * feats : (j + 1) * feats, :] = part[...]


def exact_add(total, lost, term):
    added = total + term
    seen = added - total
    return added, lost + ((total - (added - seen)) + (term - seen))


def partial_kernel(count, *refs):
    encs, inputs_ref, outs, full = refs[:count], refs[count], refs[count + 1 : -1], refs[-1]
    feats = encs[0].shape[0]
    for j in range(count):
        full[j * feats : (j + 1) * feats, :] = encs[j][...]
    upper = full[...].astype(jnp.bfloat16)
    rest = full[...] - upper.astype(jnp.float32)
    middle = rest.astype(jnp.bfloat16)
    lower = (rest - middle.astype(jnp.float32)).astype(jnp.bfloat16)
    total, lost = None, 0.0
    for cols in blocks_of(full.shape[1], 256):
        right = inputs_ref[cols, :]
        term, fine, finest = (
            jnp.dot(left[:, cols], right, preferred_element_type=jnp.float32)
            for left in (upper, middle, lower)
        )
        lost = lost + (fine + finest)
        if total is None:
            total = term
        else:
            total, lost = exact_add(total, lost, term)
    total = total + lost
    for j in range(count):
        outs[j][...] = total[j * feats : (j + 1) * feats, :]


def codes_kernel(count, *refs):
    parts, bias_ref, mask_ref, codes_ref, coded_ref = refs[:count], *refs[count:]
    pre, lost = parts[0][...], 0.0
    for part in parts[1:]:
        pre, lost = exact_add(pre, lost, part[...])
    pre, lost = exact_add(pre, lost, jnp.broadcast_to(bias_ref[...], pre.shape))
    pre = pre + lost
    codes = jnp.maximum(pre, 0.0) * mask_ref[...]
    codes_ref[...] = codes
    code_into(coded_ref, slice(None), codes)


def weights_kernel(count, feats, starts, *refs):
    parts = len(starts)
    fars, refs = refs[: parts * count], refs[parts * count :]
    (up_ref, low_ref), (*buffers, full, arrive) = refs[:2], refs[2:]
    held = Fetched(fars, buffers, arrive)
    for part, (start, stop) in enumerate(starts):
        for j in range(count):
            weights = held[part * count + j]
            for k in range(start, stop):
                row = ((k - starts[0][0]) * count + j) * feats
                rows = slice((k - start) * feats, (k - start + 1) * feats)
                full[row : row + feats, :] = decoded(weights, rows)
    for rows in blocks_of(full.shape[0], 32):
        up_ref[rows, :], low_ref[rows, :] = split(full[rows, :])


def main_kernel(count, reach, feats, starts, pieces, lates, *refs):
    fetched = count * len(lates)
    sources = count + reach - 1 + 2 * len(pieces) + fetched + 2
    results = reach + len(starts) * count
    fars, far_outs, sum_ref = refs[:sources], refs[sources : sources + results], refs[sources + results]
    refs = refs[sources + results + 1 :]
    plain = count + reach - 1
    buffers, refs = refs[: plain + fetched + 2], refs[plain + fetched + 2 :]
    outs, refs = refs[:results], refs[results:]
    full, grad, w_up, w_low, res_up, res_low, src_up, src_low, arrive, leave = refs
    block = count * feats
    places = [pl.ds(start * block, (stop - start) * block) for start, stop in pieces]
    rooms = [ref.at[place] for place in places for ref in (w_up, w_low)]
    held = Fetched(fars, [*buffers[:plain], *rooms, *buffers[plain:]], arrive)
    sends = [
        pltpu.make_async_copy(source, out, leave.at[i])
        for i, (source, out) in enumerate(zip(outs, far_outs, strict=True))
    ]
    for j in range(count):
        full[j * feats : (j + 1) * feats, :] = decoded(held[j], slice(None))
    for k in range(1, reach):
        moved = held[count + k - 1]
        for rows in blocks_of(block, 32):
            full[k * block + rows.start : k * block + rows.stop, :] = decoded(moved, rows)
    for rows in blocks_of(reach * block, 32):
        src_up[rows, :], src_low[rows, :] = split(full[rows, :])
    for i in range(2 * len(pieces)):
        held[plain + i]
    for part, (start, stop) in enumerate(lates):
        for j in range(count):
            weights = held[plain + 2 * len(pieces) + part * count + j]
            for k in range(start, stop):
                row = (k * count + j) * feats
                rows = slice((k - start) * feats, (k - start + 1) * feats)
                grad[row : row + feats, :] = decoded(weights, rows)
        for rows in blocks_of((stop - start) * block, 32):
            rows = slice(start * block + rows.start, start * block + rows.stop)
            w_up[rows, :], w_low[rows, :] = split(grad[rows, :])
    bias_ref, targets_ref = held[sources - 2], held[sources - 1]
    width, row_count = targets_ref.shape
    for cols in blocks_of(width, 256):
        recon = product(
            (w_up[:, cols], w_low[:, cols]), (src_up[...], src_low[...]), ((0,), (0,))
        )
        resid = recon + bias_ref[cols, :] - targets_ref[cols, :].astype(jnp.float32)
        sum_ref[cols, :] = jnp.sum(resid, axis=1, keepdims=True)
        res_up[cols, :], res_low[cols, :] = split(resid)
    for cols in blocks_of(row_count, 256):
        full[:, cols] = product(
            (w_up[...], w_low[...]), (res_up[:, cols], res_low[:, cols]), ((1,), (0,))
        )
    outs[0][...] = full[0:block, :]
    sends[0].start()
    for k in range(1, reach):
        for rows in blocks_of(block, 32):
            source = slice(k * block + rows.start, k * block + rows.stop)
            code_into(outs[k], rows, full[source, :])
        sends[k].start()
    for part, (start, stop) in enumerate(starts):
        held_rows = slice(start * block, stop * block)
        for rows in blocks_of(width, 256):
            grad[held_rows, rows] = product(
                (src_up[held_rows, :], src_low[held_rows, :]),
                (res_up[rows, :], res_low[rows, :]),
                ((1,), (1,)),
            )
        for j in range(count):
            place = reach + part * count + j
            for k in range(start, stop):
                row = (k * count + j) * feats
                rows = slice((k - start) * feats, (k - start + 1) * feats)
                code_into(outs[place], rows, grad[row : row + feats, :])
            sends[place].start()
    for send in sends:
        send.wait()


def code_sum_kernel(count, feats, moved_count, *refs):
    codes_ref, kept_ref = refs[0], refs[-1]
    own, moved, outs = refs[1], refs[2 : 2 + moved_count], refs[2 + moved_count : -1]
    kept_ref[...] = codes_ref[...]
    for j in range(count):
        rows = slice(j * feats, (j + 1) * feats)
        total = own[rows, :]
        for ref in moved:
            total = total + decoded(ref, rows)
        if j == 0:
            outs[0][...] = total
        else:
            code_into(outs[j], slice(None), total)


def pre_grad_kernel(count, *refs):
    own, arrived, codes_ref, coded_ref, sum_ref = refs[0], refs[1:count], *refs[count:]
    total = own[...]
    for ref in arrived:
        total = total + decoded(ref, slice(None))
    pre_grad = jnp.where(codes_ref[...] > 0.0, total, 0.0)
    sum_ref[...] = jnp.sum(pre_grad, axis=1, keepdims=True)
    code_into(coded_ref, slice(None), pre_grad)


def grad_enc_kernel(count, feats, *refs):
    far, grads, refs = refs[0], refs[1 : 1 + count], refs[1 + count :]
    outs, (inputs_ref, full, grad, arrive) = refs[:count], refs[count:]
    held = Fetched([far], [inputs_ref], arrive)
    for j in range(count):
        full[j * feats : (j + 1) * feats, :] = decoded(grads[j], slice(None))
    upper, lower = split(full[...])
    inputs_ref = held[0]
    dot = functools.partial(
        lax.dot_general,
        dimension_numbers=(((1,), (1,)), ((), ())),
        preferred_element_type=jnp.float32,
    )
    for rows in blocks_of(inputs_ref.shape[0], 256):
        right = inputs_ref[rows, :]
        grad[:, rows] = dot(upper, right) + dot(lower, right)
    for j in range(count):
        code_into(outs[j], slice(None), grad[j * feats : (j + 1) * feats, :])


def local(
    inputs,
    targets,
    enc_weight,
    enc_bias,
    dec_weight,
    dec_bias,
    enc_moments,
    enc_bias_moments,
    dec_moments,
    dec_bias_moments,
    block_lists,
    block_counts,
    slot_block,
):
    inputs_local = inputs[0]
    targets_local = targets[0]
    enc_local = enc_weight[0]
    encb_local = enc_bias[0]
    dec_local = dec_weight[0]
    decb_local = dec_bias[0]
    reach = dec_local.shape[0]
    width, row_count = inputs_local.shape
    feats = enc_local.shape[0]
    count = lax.axis_size("feat")
    block = count * feats
    depth = reach * block
    tile_count = block_counts.shape[1]
    tile_rows = row_count // tile_count
    live = jnp.arange(block_lists.shape[2])[None, :] < block_counts[0][:, None]
    hits = (block_lists[0] == slot_block[0]) & live
    tile_active = jnp.any(hits, axis=1).astype(jnp.float32)
    row_mask = jnp.repeat(tile_active, tile_rows, axis=0)[None, :]

    enc_cols = [rotated(slab_of(enc_local, j, width), j) for j in range(count)]
    me = lax.axis_index("feat").astype(jnp.int32).reshape(1)
    half_way = max(1, reach // 2)
    sent = packed(me, dec_local, 0, half_way)
    early = [rotated(sent[j], j) for j in range(count)]
    partial = call(
        functools.partial(partial_kernel, count),
        [shape(feats, row_count)] * count,
        [*enc_cols, inputs_local],
        flops=6 * block * width * row_count,
        scratch=[pltpu.VMEM((block, width), jnp.float32)],
    )
    partials = [rotated(partial[j], -j) for j in range(count)]
    codes, coded_codes = call(
        functools.partial(codes_kernel, count),
        [shape(feats, row_count), coded_shape(feats, row_count)],
        [*partials, encb_local[:, None], row_mask],
        after=early[1:],
    )
    own = [rotated(coded_codes, j) for j in range(count)]
    half = jnp.bfloat16

    def weights_of(starts, columns):
        rows = (starts[-1][1] - starts[0][0]) * block
        return call(
            functools.partial(weights_kernel, count, feats, starts),
            [shape(rows, width, half)] * 2,
            [],
            scratch=[buffer_like(a) for a in columns]
            + [pltpu.VMEM((rows, width), jnp.float32), pltpu.SemaphoreType.DMA((len(columns),))],
            far=columns,
        )

    pieces = [(0, half_way)]
    weights = [*weights_of(pieces, early)]
    gathered = call(gather_kernel, [coded_shape(block, row_count)], own, after=weights[:1])[0]
    moved = [shifted(gathered, "layer", k) for k in range(1, reach)]
    late, lates = [], [(half_way, reach)] if half_way < reach else []
    for first, last in lates:
        sent = packed(me, dec_local, first, last, after=[coded_codes])
        late += [rotated(sent[j], j, first) for j in range(count)]
    backs = (*pieces, *lates)
    far = [*own, *moved, *weights, *late, decb_local[:, None], targets_local]
    far_out = [shape(block, row_count)] + [coded_shape(block, row_count)] * (reach - 1)
    for first, last in backs:
        far_out += [coded_shape((last - first) * feats, width)] * count
    outs = call(
        functools.partial(main_kernel, count, reach, feats, backs, pieces, lates),
        [shape(width, 1)],
        [],
        flops=18 * depth * width * row_count,
        scratch=[buffer_like(a) for a in [*own, *moved, *late, *far[-2:], *far_out]]
        + [pltpu.VMEM((depth, row_count), jnp.float32), pltpu.VMEM((depth, width), jnp.float32)]
        + [pltpu.VMEM((depth, width), half)] * 2
        + [pltpu.VMEM((width, row_count), half)] * 2
        + [pltpu.VMEM((depth, row_count), half)] * 2
        + [pltpu.SemaphoreType.DMA((len(far),)), pltpu.SemaphoreType.DMA((len(far_out),))],
        far=far,
        far_out=far_out,
    )
    part, parts, grad_parts, grad_dec_bias = outs[0], outs[1:reach], outs[reach:-1], outs[-1]
    returned = [shifted(parts[k - 1], "layer", -k) for k in range(1, reach)]
    grad_dec_cols = [
        [rotated(grad_parts[i * count + j], -j, first if i else 0) for j in range(count)]
        for i, (first, last) in enumerate(backs)
    ]
    sums = call(
        functools.partial(code_sum_kernel, count, feats, reach - 1),
        [shape(feats, row_count)]
        + [coded_shape(feats, row_count)] * (count - 1)
        + [shape(feats, row_count)],
        [codes, part, *returned],
    )
    arrived = [rotated(sums[j], -j) for j in range(count)]
    coded_grad, grad_enc_bias = call(
        functools.partial(pre_grad_kernel, count),
        [coded_shape(feats, row_count), shape(feats, 1)],
        [*arrived, sums[-1]],
        after=grad_dec_cols[0][1:],
    )
    dec_done = adam_call(
        me, *backs[0], grad_dec_cols[0], dec_local, dec_moments[:, 0], after=[coded_grad]
    )
    pre_grads = [rotated(coded_grad, j) for j in range(count)]
    grad_enc_cols = call(
        functools.partial(grad_enc_kernel, count, feats),
        [coded_shape(feats, width)] * count,
        pre_grads,
        flops=4 * block * width * row_count,
        scratch=[
            buffer_like(inputs_local),
            pltpu.VMEM((block, row_count), jnp.float32),
            pltpu.VMEM((block, width), jnp.float32),
            pltpu.SemaphoreType.DMA((1,)),
        ],
        after=dec_done[:1],
        far=[inputs_local],
        alone=False,
    )
    for (first, last), grads in zip(backs[1:], grad_dec_cols[1:]):
        dec_done = adam_call(
            me, first, last, grads, dec_local, dec_moments[:, 0], dec_done, [grad_enc_cols[0]]
        )
    dec_new, dec_mom = dec_done
    enc_arrived = [rotated(grad_enc_cols[j], -j) for j in range(count)]
    enc_new, enc_mom = call(
        functools.partial(adam_kernel, count),
        [
            jax.ShapeDtypeStruct((1, *enc_local.shape), enc_local.dtype),
            jax.ShapeDtypeStruct(enc_moments.shape, enc_moments.dtype),
        ],
        [me, *enc_arrived, enc_local[None], enc_moments],
    )
    encb_new, encb_mom = adam_update(encb_local, enc_bias_moments[:, 0], grad_enc_bias[:, 0])
    decb_new, decb_mom = adam_update(decb_local, dec_bias_moments[:, 0], grad_dec_bias[:, 0])
    return (
        enc_new,
        encb_new[None],
        dec_new[None],
        decb_new[None],
        enc_mom,
        encb_mom[:, None],
        dec_mom[:, None],
        decb_mom[:, None],
    )


def solution(mesh):
    cols = P(("group", "layer"), "feat", None)
    vec = P(("group", "layer"), "feat")
    dec = P(("group", "layer"), None, "feat", None)
    cols_mom = P(None, ("group", "layer"), "feat", None)
    vec_mom = P(None, ("group", "layer"), "feat")
    dec_mom = P(None, ("group", "layer"), None, "feat", None)
    return jax.shard_map(
        local,
        mesh=mesh,
        in_specs=(
            cols,
            cols,
            cols,
            vec,
            dec,
            vec,
            cols_mom,
            vec_mom,
            dec_mom,
            vec_mom,
            P(("group", "layer"), None, None),
            P(("group", "layer"), None),
            P(("group", "layer")),
        ),
        out_specs=(cols, vec, dec, vec, cols_mom, vec_mom, dec_mom, vec_mom),
        check_vma=False,
    )
```
